32 devices in a mesh: group: 2 (over y), seq: 4 (over z), fsdp: 4 (over x, core).
Axes of the slice: x: 2, y: 2, z: 4, core: 2. Of those that a mesh axis runs over, the one named last changes fastest.
Arguments:
- tile_patches: bfloat16 [64, 256, 1536], P(('group', 'seq', 'fsdp')), parts along dimension 0, may hold values from -6 to 6
- vit_gain: float32 [1536], replicated, may hold values from 0.25 to 1.75
- w_query: bfloat16 [1536, 768], P('fsdp'), may hold values from -0.15625 to 0.15625
- w_key: bfloat16 [1536, 768], P('fsdp'), may hold values from -0.15625 to 0.15625
- w_value: bfloat16 [1536, 768], P('fsdp'), may hold values from -0.15625 to 0.15625
- w_out: bfloat16 [768, 1536], P('fsdp'), may hold values from -0.21875 to 0.21875
- w_proj: bfloat16 [1536, 768], P('fsdp'), may hold values from -0.15625 to 0.15625
- long_gain: float32 [768], replicated, may hold values from 0.25 to 1.75
- long_query: bfloat16 [768, 768], P(None, 'fsdp'), may hold values from -0.21875 to 0.21875
- long_key: bfloat16 [768, 768], P(None, 'fsdp'), may hold values from -0.21875 to 0.21875
- long_value: bfloat16 [768, 768], P(None, 'fsdp'), may hold values from -0.21875 to 0.21875
- long_out: bfloat16 [768, 768], P('fsdp'), may hold values from -0.21875 to 0.21875
- seq_order: int32 [64], P(('group', 'seq', 'fsdp')), parts along dimension 0, may hold values from 0 to 31, each once
- counts: int32 [32], P(('group', 'seq', 'fsdp')), parts along dimension 0, may hold values from 1 to 2
Outputs:
- encoded: bfloat16 [64, 768], P(('group', 'seq'), 'fsdp'), parts along dimension 0
The draws below stay inside these ranges and needn't reach their ends.
There are 2 independent parts, one for each index of `group`. The reference program is written for one: setup_inputs(seed, part) draws one part's arguments, and reference() takes and returns one part's arrays. A program takes and returns all parts, laid end to end along the dimension named above; an argument that names none is the same for every part. Nothing has to cross between parts.
Inputs may be any that keep to these rules, and one draw needn't show every extreme that they name: `seq_order`: each of the 32 sequence positions belongs to exactly one tile. In each block of 2 consecutive tiles the first counts tiles are tissue.
All inputs are finite; a program needn't handle non-finite values.
Results may differ from the reference program's by a relative error of at most 0.013.
Values may be sent and summed in bfloat16 or wider, within the bound.
A program may use at most 64 MiB of HBM per device.

```python
import math
import jax
import jax.numpy as jnp
from jax import lax

DV = 1536
VH = 12
VHD = 64
PATCH = 256
TILE_DEV = 2
D = 768
HEADS = 16
DILATION_STEP = 4
TILES = 32
N_SEQ = 4
N_FSDP = 4


def touch_ends(entries, own_key, smallest, top_value):
    dims = entries.shape
    spot = [jax.random.randint(jax.random.fold_in(own_key, axis), (), 0, dims[axis]) for axis in range(len(dims))]
    entries = entries.at[tuple(spot)].set(smallest)
    longest = dims.index(max(dims))
    spot[longest] = (spot[longest] + 1) % dims[longest]
    return entries.at[tuple(spot)].set(top_value)


def level_of(rng, shape, cuts, smallest, top_value):
    def one(axis_at, blocks):
        draws = jax.random.uniform(jax.random.fold_in(jax.random.fold_in(rng, 6), axis_at), (blocks,), jnp.float32, smallest / len(cuts), top_value / len(cuts))
        return jnp.repeat(jnp.exp(draws), shape[axis_at] // blocks).reshape((-1,) + (1,) * (len(shape) - axis_at - 1))

    loudness = one(*cuts[0])
    for cut in cuts[1:]:
        loudness = loudness * one(*cut)
    return loudness


def scatter_about(rng, shape, width, reach, shards=(), kind=jnp.bfloat16):
    gain = level_of(rng, shape, shards, -0.22, 0.18) if shards else 1.0
    array = jax.random.normal(rng, shape, jnp.float32) * width * gain
    return jnp.minimum(jnp.maximum(array, -reach), reach).astype(kind)


def setup_inputs(seed: int = 0, part: int = 0) -> dict:
    keys = jax.random.split(jax.random.key(seed), 15)
    part_keys = jax.random.split(jax.random.fold_in(keys[14], part), 15)
    tile_patches = scatter_about(part_keys[0], (TILES, PATCH, DV), 1.0, 6.0, ((0, 16),))
    vit_gain = jnp.clip(1.0 + 0.15 * jax.random.normal(keys[1], (DV,), jnp.float32), 0.25, 1.75)
    w_query = scatter_about(keys[2], (DV, VH * VHD), DV ** -0.5, 0.15625, ((0, 4),))
    w_key = scatter_about(keys[3], (DV, VH * VHD), DV ** -0.5, 0.15625, ((0, 4),))
    w_value = scatter_about(keys[4], (DV, VH * VHD), DV ** -0.5, 0.15625, ((0, 4),))
    w_out = scatter_about(keys[5], (VH * VHD, DV), (VH * VHD) ** -0.5, 0.21875, ((0, 4),))
    w_proj = scatter_about(keys[6], (DV, D), DV ** -0.5, 0.15625, ((0, 4),))
    long_gain = jnp.clip(1.0 + 0.15 * jax.random.normal(keys[7], (D,), jnp.float32), 0.25, 1.75)
    long_query = scatter_about(keys[8], (D, D), D ** -0.5, 0.21875, ((1, 4),))
    long_key = scatter_about(keys[9], (D, D), D ** -0.5, 0.21875, ((1, 4),))
    long_value = scatter_about(keys[10], (D, D), D ** -0.5, 0.21875, ((1, 4),))
    long_out = scatter_about(keys[11], (D, D), D ** -0.5, 0.21875, ((0, 4),))
    seq_order = jax.random.permutation(part_keys[12], TILES).astype(jnp.int32)
    counts = touch_ends(jax.random.randint(part_keys[13], (N_SEQ * N_FSDP,), 1, TILE_DEV + 1), jax.random.fold_in(part_keys[13], 1), 1, TILE_DEV).astype(jnp.int32)
    return {"tile_patches": tile_patches, "vit_gain": vit_gain, "w_query": w_query, "w_key": w_key, "w_value": w_value, "w_out": w_out, "w_proj": w_proj, "long_gain": long_gain, "long_query": long_query, "long_key": long_key, "long_value": long_value, "long_out": long_out, "seq_order": seq_order, "counts": counts}


EPSILON = 1e-06

def layer_norm(inputs, norm_gain):
    widened = inputs.astype(jnp.float32)
    average = lax.optimization_barrier(jnp.mean(widened, axis=-1, keepdims=True))
    centred = widened - average
    variance = lax.optimization_barrier(jnp.mean(centred * centred, axis=-1, keepdims=True))
    return (centred * lax.rsqrt(variance + EPSILON) * norm_gain).astype(jnp.bfloat16)

def dilated_attention(query_rows, key_rows, value_rows, query_position_index, key_position_index, key_present, leading_head, head_total_count, segment):
    head_size = query_rows.shape[1] // head_total_count
    query_heads = query_rows.reshape(query_rows.shape[0], head_total_count, head_size).astype(jnp.float32)
    key_heads = key_rows.reshape(key_rows.shape[0], head_total_count, head_size).astype(jnp.float32)
    value_heads = value_rows.reshape(value_rows.shape[0], head_total_count, head_size).astype(jnp.float32)
    scores = jnp.einsum('rhd,khd->hrk', query_heads, key_heads) / math.sqrt(head_size)
    itself = query_position_index[:, None] == key_position_index[None, :]
    permitted_mask = (key_present[None, :] > 0) | itself
    in_local = (query_position_index[:, None] // segment == key_position_index[None, :] // segment) & permitted_mask
    head_shift_amounts = (leading_head + jnp.arange(head_total_count, dtype=jnp.int32)) % DILATION_STEP
    within_dilated_set = ((query_position_index % DILATION_STEP)[None, :, None] == head_shift_amounts[:, None, None]) & ((key_position_index % DILATION_STEP)[None, None, :] == head_shift_amounts[:, None, None]) & permitted_mask[None]
    lifted = jnp.exp(scores)
    local_weights = jnp.where(in_local[None], lifted, 0.0)
    dilated_weights = jnp.where(within_dilated_set, lifted, 0.0)
    denominator = lax.optimization_barrier(jnp.sum(local_weights, axis=-1)) + lax.optimization_barrier(jnp.sum(dilated_weights, axis=-1))
    numerator = jnp.einsum('hrk,khd->rhd', local_weights.astype(jnp.bfloat16).astype(jnp.float32), value_heads)
    numerator = numerator + jnp.einsum('hrk,khd->rhd', dilated_weights.astype(jnp.bfloat16).astype(jnp.float32), value_heads)
    combined = numerator / jnp.transpose(denominator)[:, :, None]
    return combined.reshape(query_rows.shape[0], head_total_count * head_size).astype(jnp.bfloat16)

def reference(tile_patches, vit_gain, w_query, w_key, w_value, w_out, w_proj, long_gain, long_query, long_key, long_value, long_out, seq_order, counts):

    def encode(one_tile):
        normed = layer_norm(one_tile, vit_gain)
        key_rows = jnp.dot(normed, w_key, preferred_element_type=jnp.float32)
        value_rows = jnp.dot(normed, w_value, preferred_element_type=jnp.float32)
        query_row = jnp.dot(normed[0:1], w_query, preferred_element_type=jnp.float32).astype(jnp.bfloat16)
        query_heads = query_row.reshape(VH, VHD).astype(jnp.float32)
        key_heads = key_rows.reshape(PATCH, VH, VHD)
        scores = jnp.einsum('hd,phd->hp', query_heads, key_heads, precision=lax.Precision.HIGHEST) / math.sqrt(VHD)
        lifted = jnp.exp(scores)
        attn_probs = (lifted / lax.optimization_barrier(jnp.sum(lifted, axis=-1, keepdims=True))).astype(jnp.bfloat16)
        value_heads = value_rows.reshape(PATCH, VH, VHD)
        pooled = jnp.einsum('hp,phd->hd', attn_probs.astype(jnp.float32), value_heads, precision=lax.Precision.HIGHEST).reshape(1, VH * VHD).astype(jnp.bfloat16)
        class_row = (one_tile[0:1].astype(jnp.float32) + jnp.dot(pooled, w_out, preferred_element_type=jnp.float32)).astype(jnp.bfloat16)
        return jnp.dot(class_row, w_proj, preferred_element_type=jnp.float32)[0].astype(jnp.bfloat16)
    embeds = lax.map(encode, tile_patches)
    tile_index = jnp.arange(TILES, dtype=jnp.int32)
    present = (tile_index % TILE_DEV < counts[tile_index // TILE_DEV]).astype(jnp.int32)
    embeds = jnp.where(present[:, None] > 0, embeds, jnp.zeros_like(embeds))
    sequence = jnp.zeros((TILES, D), jnp.bfloat16).at[seq_order].set(embeds)
    seq_present = jnp.zeros((TILES,), jnp.int32).at[seq_order].set(present)
    long_normed = layer_norm(sequence, long_gain)
    query_rows = jnp.dot(long_normed, long_query, preferred_element_type=jnp.float32).astype(jnp.bfloat16)
    key_rows = jnp.dot(long_normed, long_key, preferred_element_type=jnp.float32).astype(jnp.bfloat16)
    value_rows = jnp.dot(long_normed, long_value, preferred_element_type=jnp.float32).astype(jnp.bfloat16)
    positions = jnp.arange(TILES, dtype=jnp.int32)
    attended = dilated_attention(query_rows, key_rows, value_rows, positions, positions, seq_present, 0, HEADS, TILES // 4)
    return (sequence.astype(jnp.float32) + jnp.dot(attended, long_out, preferred_element_type=jnp.float32)).astype(jnp.bfloat16)
```

```python
import functools
import math

import jax
import jax.numpy as jnp
from jax import lax
from jax.experimental import pallas as pl
from jax.experimental.pallas import tpu as pltpu
from jax.sharding import PartitionSpec as P

VHD = 64
HEADS = 16
DILATION_STEP = 4
EPSILON = 1e-06
LN_ROWS = 32

F32 = jnp.float32
BF16 = jnp.bfloat16


def up(n, m):
    return (n + m - 1) // m * m


def norm_rows(x, gain):
    mean = jnp.mean(x, axis=-1, keepdims=True)
    centred = x - mean
    variance = jnp.mean(centred * centred, axis=-1, keepdims=True)
    return centred * lax.rsqrt(variance + EPSILON) * gain


def dot(a, b):
    return jnp.dot(a, b, preferred_element_type=F32)


def dot_t(a, b):
    return lax.dot_general(a, b, (((1,), (1,)), ((), ())), preferred_element_type=F32)


def kernel(
    F, S,
    patches, vit_gain, w_query, w_key, w_value, w_out, w_proj,
    long_gain, long_query, long_key, long_value, long_out, order, counts,
    out,
    cls, xbuf, normed, wq, wk, wv, wo, wp, lq, lk, lv, lo,
    s1, r1, sm, rm, sm2, rm2, s2, r2, s3, r3, s4, r4, s5, r5, s6, r6, s7, r7,
    s8, r8, s9, r9, qbuf, seqc,
    lsem, fsend, frecv, zsend, zrecv,
):
    T, PATCH, DV = patches.shape
    VW = w_key.shape[1]
    D = w_proj.shape[1]
    R = T * F
    N = R * S
    C = DV // F
    HC = long_query.shape[1]
    OC = D // F
    PC = VW // F
    HP = up(VW // VHD, 16)
    f = lax.axis_index("fsdp")
    z = lax.axis_index("seq")

    loads = []

    def load(src, dst):
        c = pltpu.make_async_copy(src, dst, lsem.at[len(loads)])
        c.start()
        loads.append(c)
        return c

    ld_cls = load(patches.at[:, pl.ds(0, 16), :], cls)
    barrier = pltpu.get_barrier_semaphore()
    for k in range(1, F):
        pl.semaphore_signal(
            barrier, inc=1, device_id={"fsdp": lax.rem(f + k, F)},
            device_id_type=pl.DeviceIdType.MESH)
    for k in range(1, S):
        pl.semaphore_signal(
            barrier, inc=1, device_id={"seq": lax.rem(z + k, S)},
            device_id_type=pl.DeviceIdType.MESH)
    ld_wq = load(w_query, wq)
    ld_x = [load(patches.at[t], xbuf.at[t]) for t in range(T)]
    ld_wk = load(w_key, wk)
    ld_wv = load(w_value, wv)
    ld_wo = load(w_out, wo)
    ld_wp = load(w_proj, wp)
    ld_lq = load(long_query, lq)
    ld_lk = load(long_key, lk)
    ld_lv = load(long_value, lv)
    ld_lo = load(long_out, lo)

    sends = []

    def push(hop, axis, me, n, src, dst, send_sems, recv_sems):
        for k in sorted(range(1, n), key=lambda k: abs(2 * k - n)):
            peer = lax.rem(me + k, n)
            c = pltpu.make_async_remote_copy(
                src_ref=src(peer), dst_ref=dst.at[me],
                send_sem=send_sems.at[hop, k], recv_sem=recv_sems.at[hop, me],
                device_id={axis: peer}, device_id_type=pl.DeviceIdType.MESH)
            c.start()
            sends.append(c)

    def collect(hop, axis, me, n, dst, send_sems, recv_sems):
        for k in range(1, n):
            peer = lax.rem(me + k, n)
            pltpu.make_async_remote_copy(
                src_ref=dst.at[me], dst_ref=dst.at[peer],
                send_sem=send_sems.at[hop, k], recv_sem=recv_sems.at[hop, peer],
                device_id={axis: peer}, device_id_type=pl.DeviceIdType.MESH,
            ).wait_recv()

    def scatter(hop, src, dst):
        push(hop, "fsdp", f, F, lambda peer: src.at[peer], dst, fsend, frecv)
        dst[f] = src[f]

    def spread(hop, src, dst):
        push(hop, "fsdp", f, F, lambda peer: src, dst, fsend, frecv)
        dst[f] = src[...]

    def spread_z(hop, src, dst):
        push(hop, "seq", z, S, lambda peer: src, dst, zsend, zrecv)
        dst[z] = src[...]

    def arrive(hop, dst):
        collect(hop, "fsdp", f, F, dst, fsend, frecv)

    def arrive_z(hop, dst):
        collect(hop, "seq", z, S, dst, zsend, zrecv)

    def total(ref, n):
        acc = ref[0]
        for j in range(1, n):
            acc = acc + ref[j]
        return acc

    L = sm.shape[1]
    lane = lax.broadcasted_iota(jnp.int32, sm.shape, 1)
    row = lax.broadcasted_iota(jnp.int32, sm.shape, 0)
    meta = jnp.zeros(sm.shape, jnp.int32)
    first = z * R + f * T
    for t in range(T):
        here = jnp.where(t < counts[0], 1, 0)
        value = jnp.where(row == 0, order[t] + 1, jnp.where(row == 1, here, 0))
        meta = jnp.where(lane == first + t, value, meta)
    sm[...] = meta

    ld_cls.wait()
    raw = jnp.concatenate([cls[t, 0:8, :].astype(F32)[0:1] for t in range(T)], axis=0)
    class_normed = norm_rows(raw, vit_gain[...]).astype(BF16).astype(F32)
    filler = s1.shape[1] - 2 * T
    packed = jnp.concatenate(
        [class_normed, raw, jnp.zeros((filler, DV), F32)], axis=0)
    for j in range(F):
        s1[j] = packed[:, j * C:(j + 1) * C]
    pl.semaphore_wait(barrier, F - 1 + S - 1)
    scatter(0, s1, r1)
    spread(1, sm, rm)

    blocks = PATCH // LN_ROWS

    def norm_blocks(lo_block, hi_block):
        def body(i, carry):
            t = i // blocks
            start = pl.multiple_of((i % blocks) * LN_ROWS, LN_ROWS)
            x = xbuf[t, pl.ds(start, LN_ROWS), :].astype(F32)
            y = norm_rows(x, vit_gain[...])
            for j in range(F):
                normed[t, j, pl.ds(start, LN_ROWS), :] = y[:, j * C:(j + 1) * C].astype(BF16)
            return carry
        lax.fori_loop(lo_block, hi_block, body, 0)

    third = T * blocks // 3
    for c in ld_x:
        c.wait()
    norm_blocks(0, third)

    ld_wq.wait()
    arrive(0, r1)
    xq = jnp.concatenate([r1[j][0:T] for j in range(F)], axis=0)
    s2[...] = dot(xq.astype(BF16), wq[...])
    spread(2, s2, r2)
    arrive(1, rm)
    sm2[...] = total(rm, F)
    spread_z(0, sm2, rm2)
    norm_blocks(third, 2 * third)
    ld_wk.wait()
    arrive(2, r2)
    query = total(r2, F).astype(BF16).astype(F32)

    head = lax.broadcasted_iota(jnp.int32, (R, HP, VW), 1)
    column = lax.broadcasted_iota(jnp.int32, (R, HP, VW), 2)
    own_head = (column >= head * VHD) & (column < (head + 1) * VHD)
    spread_query = jnp.where(own_head, query[:, None, :], 0.0).reshape(R * HP, VW)
    folded = dot_t(spread_query.astype(BF16), wk[...]).astype(BF16)
    s3[...] = folded.reshape(F, T * HP, C)
    scatter(3, s3, r3)
    norm_blocks(2 * third, T * blocks)
    arrive(3, r3)

    for t in range(T):
        scores = dot_t(r3[0, pl.ds(t * HP, HP), :], normed[t, 0])
        for j in range(1, F):
            scores = scores + dot_t(r3[j, pl.ds(t * HP, HP), :], normed[t, j])
        lifted = jnp.exp(scores / math.sqrt(VHD))
        probs = (lifted / jnp.sum(lifted, axis=-1, keepdims=True)).astype(BF16)
        for j in range(F):
            s4[j, pl.ds(t * HP, HP), :] = dot(probs, normed[t, j]).astype(BF16)
    scatter(4, s4, r4)
    ld_wv.wait()
    ld_wo.wait()
    arrive(4, r4)

    summed = dot(r4[...].reshape(R * HP, C), wv[...]).reshape(R, HP, VW)
    pooled_part = jnp.sum(jnp.where(own_head, summed, 0.0), axis=1)
    for j in range(F):
        s5[j] = pooled_part[:, j * PC:(j + 1) * PC]
    scatter(5, s5, r5)
    arrive(5, r5)
    pooled = total(r5, F).astype(BF16)
    row_part = dot(pooled, wo[...])
    for j in range(F):
        s6[j] = row_part[:, j * C:(j + 1) * C]
    scatter(6, s6, r6)
    class_raw = jnp.concatenate([r1[j][T:2 * T] for j in range(F)], axis=0)
    ld_wp.wait()
    arrive(6, r6)
    class_row = (class_raw + total(r6, F)).astype(BF16)
    s7[...] = dot(class_row, wp[...])
    spread(7, s7, r7)

    arrive_z(0, rm2)
    all_meta = total(rm2, S)
    all_order = all_meta[0:1, 0:N]
    all_present = all_meta[1:2, 0:N].astype(F32)
    position = lax.broadcasted_iota(jnp.int32, (N, N), 0) + 1
    picker = jnp.where(position == all_order, 1.0, 0.0)
    picker_tissue = (picker * all_present).astype(BF16)
    key_present = dot_t(jnp.broadcast_to(all_present, (8, N)).astype(BF16), picker.astype(BF16))[0:1]

    arrive(7, r7)
    embeds = total(r7, F).astype(BF16).astype(F32)
    half = D // 2
    s8[...] = jnp.concatenate([embeds[:, :half], embeds[:, half:]], axis=0).astype(BF16)
    spread_z(1, s8, r8)
    heads_dev = HC // (D // HEADS)
    hw = D // HEADS
    hr = (heads_dev, R, N)
    m_head = lax.broadcasted_iota(jnp.int32, hr, 0) + f * heads_dev
    m_row = lax.broadcasted_iota(jnp.int32, hr, 1) + z * R
    m_key = lax.broadcasted_iota(jnp.int32, hr, 2)
    segment = N // 4
    allowed = (key_present.reshape(1, 1, N) > 0.5) | (m_row == m_key)
    in_local = m_row // segment == m_key // segment
    in_dilated = (m_row % DILATION_STEP == m_head % DILATION_STEP) & (
        m_key % DILATION_STEP == m_head % DILATION_STEP)
    times = jnp.where(
        allowed, jnp.where(in_local, 1.0, 0.0) + jnp.where(in_dilated, 1.0, 0.0), 0.0
    ).reshape(heads_dev * R, N)
    a_head = lax.broadcasted_iota(jnp.int32, (heads_dev, R, HC), 0)
    a_col = lax.broadcasted_iota(jnp.int32, (heads_dev, R, HC), 2)
    mine = (a_col >= a_head * hw) & (a_col < (a_head + 1) * hw)
    ld_lq.wait()
    ld_lk.wait()
    ld_lv.wait()
    ld_lo.wait()
    arrive_z(1, r8)

    left = jnp.concatenate([r8[j].astype(F32)[:R] for j in range(S)], axis=0)
    right = jnp.concatenate([r8[j].astype(F32)[R:] for j in range(S)], axis=0)
    every = jnp.concatenate([left, right], axis=1).astype(BF16)
    sequence = dot(picker_tissue, every)
    lnormed = norm_rows(sequence, long_gain[...]).astype(BF16)
    qbuf[...] = dot(lnormed, lq[...])
    keys = dot(lnormed, lk[...]).astype(BF16)
    values = dot(lnormed, lv[...]).astype(BF16)
    queries = qbuf[pl.ds(pl.multiple_of(z * R, R), R), :].astype(BF16).astype(F32)
    per_head = jnp.where(mine, queries[None], 0.0).reshape(heads_dev * R, HC).astype(BF16)
    lifted = jnp.exp(dot_t(per_head, keys) / math.sqrt(hw))
    weights = lifted.astype(BF16).astype(F32) * times
    denominator = jnp.sum(lifted * times, axis=-1, keepdims=True)
    mixed = dot(weights.astype(BF16), values) / denominator
    attended = jnp.sum(
        jnp.where(mine, mixed.reshape(heads_dev, R, HC), 0.0), axis=0).astype(BF16)
    terms = dot(attended, lo[...])
    for j in range(F):
        s9[j] = terms[:, j * OC:(j + 1) * OC]
    scatter(8, s9, r9)
    for j in range(F):
        seqc[j] = sequence[:, j * OC:(j + 1) * OC]
    residual = seqc[f, pl.ds(pl.multiple_of(z * R, R), R), :]
    arrive(8, r9)
    out[...] = (residual + total(r9, F)).astype(BF16)
    for c in sends:
        c.wait_send()


def local(
    tile_patches, vit_gain, w_query, w_key, w_value, w_out, w_proj,
    long_gain, long_query, long_key, long_value, long_out, seq_order, counts,
):
    S = lax.axis_size("seq")
    F = lax.axis_size("fsdp")
    T, PATCH, DV = tile_patches.shape
    VW = w_key.shape[1]
    D = w_proj.shape[1]
    R, C, HC, OC, PC = T * F, DV // F, long_query.shape[1], D // F, VW // F
    HP = up(VW // VHD, 16)
    N = R * S
    L = up(N, 128)
    V = pltpu.VMEM
    any_, vmem, smem = (
        pl.BlockSpec(memory_space=m) for m in (pl.ANY, pltpu.VMEM, pltpu.SMEM))
    like = lambda a: V(a.shape, a.dtype)
    pair = lambda shape, dtype: [V((F,) + shape, dtype), V((F,) + shape, dtype)]
    fan = lambda n, shape, dtype: [V(shape, dtype), V((n,) + shape, dtype)]
    flops = 2 * (3 * R * HP * C * VW + 2 * T * HP * PATCH * DV + 3 * N * D * HC)
    return pl.pallas_call(
        functools.partial(kernel, F, S),
        out_shape=jax.ShapeDtypeStruct((R, OC), BF16),
        in_specs=[any_, vmem, any_, any_, any_, any_, any_, vmem,
                  any_, any_, any_, any_, smem, smem],
        out_specs=vmem,
        scratch_shapes=[
            V((T, 16, DV), BF16), like(tile_patches), V((T, F, PATCH, C), BF16),
            like(w_query), like(w_key), like(w_value), like(w_out), like(w_proj),
            like(long_query), like(long_key), like(long_value), like(long_out),
            *pair((up(2 * T, 8), C), F32),
            *fan(F, (8, L), jnp.int32),
            *fan(S, (8, L), jnp.int32),
            *fan(F, (R, VW), F32),
            *pair((T * HP, C), BF16),
            *pair((T * HP, C), BF16),
            *pair((R, PC), F32),
            *pair((R, C), F32),
            *fan(F, (R, D), F32),
            *fan(S, (2 * R, D // 2), BF16),
            *pair((R, OC), F32),
            V((N, HC), F32), V((F, N, OC), F32),
            pltpu.SemaphoreType.DMA((10 + T,)),
            pltpu.SemaphoreType.DMA((9, F)), pltpu.SemaphoreType.DMA((9, F)),
            pltpu.SemaphoreType.DMA((2, S)), pltpu.SemaphoreType.DMA((2, S)),
        ],
        compiler_params=pltpu.CompilerParams(
            collective_id=0, has_side_effects=True, vmem_limit_bytes=48 * 2**20),
        cost_estimate=pl.CostEstimate(
            flops=flops, bytes_accessed=8 * 2**20, transcendentals=T * HP * PATCH),
    )(
        tile_patches, vit_gain.reshape(1, DV), w_query, w_key, w_value, w_out, w_proj,
        long_gain.reshape(1, D), long_query, long_key, long_value, long_out,
        seq_order, counts,
    )


def solution(mesh):
    return jax.shard_map(
        local,
        mesh=mesh,
        in_specs=(
            P(("group", "seq", "fsdp"), None, None),
            P(),
            P("fsdp", None),
            P("fsdp", None),
            P("fsdp", None),
            P("fsdp", None),
            P("fsdp", None),
            P(),
            P(None, "fsdp"),
            P(None, "fsdp"),
            P(None, "fsdp"),
            P("fsdp", None),
            P(("group", "seq", "fsdp")),
            P(("group", "seq", "fsdp")),
        ),
        out_specs=P(("group", "seq"), "fsdp"),
        check_vma=False,
    )
```

```python
import functools
import math

import jax
import jax.numpy as jnp
from jax import lax
from jax.experimental import pallas as pl
from jax.experimental.pallas import tpu as pltpu
from jax.sharding import PartitionSpec as P

VHD = 64
HEADS = 16
DILATION_STEP = 4
EPSILON = 1e-06
LN_ROWS = 64

F32 = jnp.float32
BF16 = jnp.bfloat16


def stack_halves(x):
    half = x.shape[1] // 2
    return jnp.concatenate([x[:, :half], x[:, half:]], axis=0)


def join_halves(x):
    half = x.shape[0] // 2
    return jnp.concatenate([x[:half], x[half:]], axis=1)


def up(n, m):
    return (n + m - 1) // m * m


def norm_rows(x, gain):
    mean = jnp.mean(x, axis=-1, keepdims=True)
    centred = x - mean
    variance = jnp.mean(centred * centred, axis=-1, keepdims=True)
    return centred * lax.rsqrt(variance + EPSILON) * gain


def dot(a, b):
    return jnp.dot(a, b, preferred_element_type=F32)


def dot_t(a, b):
    return lax.dot_general(a, b, (((1,), (1,)), ((), ())), preferred_element_type=F32)


def kernel(
    F, S,
    patches, vit_gain, w_query, w_key, w_value, w_out, w_proj,
    long_gain, long_query, long_key, long_value, long_out, order_hbm, counts,
    out, order,
    cls, xbuf, normed, wq, wk, wv, wo, wp, lq, lk, lv, lo,
    s1, r1, sm, rm, sm2, rm2, s2, r2, s3, r3, s4, r4, s5, r5, s6, r6, s7, r7,
    s8, r8, s9, r9, qbuf, seqc,
    lsem, fsend, frecv, zsend, zrecv,
):
    T, PATCH, DV = patches.shape
    VW = w_key.shape[1]
    D = w_proj.shape[1]
    R = T * F
    N = R * S
    C = DV // F
    HC = long_query.shape[0]
    OC = D // F
    PC = VW // F
    HP = up(VW // VHD, 16)
    f = lax.axis_index("fsdp")
    z = lax.axis_index("seq")

    loads = []

    def load(src, dst):
        c = pltpu.make_async_copy(src, dst, lsem.at[len(loads)])
        c.start()
        loads.append(c)
        return c

    ld_cls = load(patches.at[:, pl.ds(0, 16), :], cls)
    barrier = pltpu.get_barrier_semaphore()
    for k in range(1, F):
        pl.semaphore_signal(
            barrier, inc=1, device_id={"fsdp": lax.rem(f + k, F)},
            device_id_type=pl.DeviceIdType.MESH)
    for k in range(1, S):
        pl.semaphore_signal(
            barrier, inc=1, device_id={"seq": lax.rem(z + k, S)},
            device_id_type=pl.DeviceIdType.MESH)
    ld_order = load(order_hbm, order)
    ld_wq = load(w_query, wq)
    ld_x = [load(patches.at[t], xbuf.at[t]) for t in range(T)]
    ld_wk = load(w_key, wk)
    ld_wv = load(w_value, wv)
    ld_wo = load(w_out, wo)
    ld_wp = load(w_proj, wp)
    ld_lq = load(long_query, lq)
    ld_lk = load(long_key, lk)
    ld_lv = load(long_value, lv)
    ld_lo = load(long_out, lo)

    sends = []

    def push(hop, axis, me, n, src, dst, send_sems, recv_sems):
        for k in sorted(range(1, n), key=lambda k: abs(2 * k - n)):
            peer = lax.rem(me + k, n)
            c = pltpu.make_async_remote_copy(
                src_ref=src(peer), dst_ref=dst.at[me],
                send_sem=send_sems.at[hop, k], recv_sem=recv_sems.at[hop, me],
                device_id={axis: peer}, device_id_type=pl.DeviceIdType.MESH)
            c.start()
            sends.append(c)

    def collect(hop, axis, me, n, dst, send_sems, recv_sems):
        for k in range(1, n):
            peer = lax.rem(me + k, n)
            pltpu.make_async_remote_copy(
                src_ref=dst.at[me], dst_ref=dst.at[peer],
                send_sem=send_sems.at[hop, k], recv_sem=recv_sems.at[hop, peer],
                device_id={axis: peer}, device_id_type=pl.DeviceIdType.MESH,
            ).wait_recv()

    def scatter(hop, src, dst):
        push(hop, "fsdp", f, F, lambda peer: src.at[peer], dst, fsend, frecv)
        dst[f] = src[f]

    def spread(hop, src, dst):
        push(hop, "fsdp", f, F, lambda peer: src, dst, fsend, frecv)
        dst[f] = src[...]

    def spread_z(hop, src, dst):
        push(hop, "seq", z, S, lambda peer: src, dst, zsend, zrecv)
        dst[z] = src[...]

    def arrive(hop, dst):
        collect(hop, "fsdp", f, F, dst, fsend, frecv)

    def arrive_z(hop, dst):
        collect(hop, "seq", z, S, dst, zsend, zrecv)

    def total(ref, n):
        part = lambda j: ref[j].astype(F32) if ref.dtype == BF16 else ref[j]
        acc = part(0)
        for j in range(1, n):
            acc = acc + part(j)
        return acc

    ld_cls.wait()
    raw = jnp.concatenate([cls[t, 0:8, :].astype(F32)[0:1] for t in range(T)], axis=0)
    class_normed = norm_rows(raw, vit_gain[...].reshape(1, DV)).astype(BF16).astype(F32)
    filler = s1.shape[1] - 2 * T
    packed = jnp.concatenate(
        [class_normed, raw, jnp.zeros((filler, DV), F32)], axis=0)
    for j in range(F):
        s1[j] = packed[:, j * C:(j + 1) * C]
    pl.semaphore_wait(barrier, F - 1 + S - 1)
    scatter(0, s1, r1)
    ld_order.wait()
    L = sm.shape[1]
    lane = lax.broadcasted_iota(jnp.int32, sm.shape, 1)
    row = lax.broadcasted_iota(jnp.int32, sm.shape, 0)
    meta = jnp.zeros(sm.shape, jnp.int32)
    first = z * R + f * T
    for t in range(T):
        here = jnp.where(t < counts[0], 1, 0)
        value = jnp.where(row == 0, order[t] + 1, jnp.where(row == 1, here, 0))
        meta = jnp.where(lane == first + t, value, meta)
    sm[...] = meta
    spread(1, sm, rm)

    blocks = PATCH // LN_ROWS

    def norm_blocks(lo_block, hi_block):
        def body(i, carry):
            t = i // blocks
            start = pl.multiple_of((i % blocks) * LN_ROWS, LN_ROWS)
            x = xbuf[t, pl.ds(start, LN_ROWS), :].astype(F32)
            y = norm_rows(x, vit_gain[...].reshape(1, DV))
            for j in range(F):
                normed[t, j, pl.ds(start, LN_ROWS), :] = y[:, j * C:(j + 1) * C].astype(BF16)
            return carry
        lax.fori_loop(lo_block, hi_block, body, 0)

    third = T * blocks // 3
    for c in ld_x:
        c.wait()
    norm_blocks(0, third)

    ld_wq.wait()
    arrive(0, r1)
    xq = jnp.concatenate([r1[j][0:T] for j in range(F)], axis=0)
    s2[...] = stack_halves(dot(xq.astype(BF16), wq[...])).astype(BF16)
    spread(2, s2, r2)
    arrive(1, rm)
    sm2[...] = total(rm, F)
    spread_z(0, sm2, rm2)
    norm_blocks(third, 2 * third)
    ld_wk.wait()
    arrive(2, r2)
    query = join_halves(total(r2, F).astype(BF16).astype(F32))

    head = lax.broadcasted_iota(jnp.int32, (R, HP, VW), 1)
    column = lax.broadcasted_iota(jnp.int32, (R, HP, VW), 2)
    own_head = (column >= head * VHD) & (column < (head + 1) * VHD)
    spread_query = jnp.where(own_head, query[:, None, :], 0.0).reshape(R * HP, VW)
    folded = dot_t(spread_query.astype(BF16), wk[...]).astype(BF16)
    s3[...] = folded.reshape(F, T * HP, C)
    scatter(3, s3, r3)
    norm_blocks(2 * third, T * blocks)
    arrive(3, r3)

    for t in range(T):
        scores = dot_t(r3[0, pl.ds(t * HP, HP), :], normed[t, 0])
        for j in range(1, F):
            scores = scores + dot_t(r3[j, pl.ds(t * HP, HP), :], normed[t, j])
        lifted = jnp.exp(scores / math.sqrt(VHD))
        probs = (lifted / jnp.sum(lifted, axis=-1, keepdims=True)).astype(BF16)
        for j in range(F):
            s4[j, pl.ds(t * HP, HP), :] = dot(probs, normed[t, j]).astype(BF16)
    scatter(4, s4, r4)
    ld_wv.wait()
    ld_wo.wait()
    arrive(4, r4)

    summed = dot(r4[...].reshape(R * HP, C), wv[...]).reshape(R, HP, VW)
    pooled_part = jnp.sum(jnp.where(own_head, summed, 0.0), axis=1)
    for j in range(F):
        s5[j] = pooled_part[:, j * PC:(j + 1) * PC]
    scatter(5, s5, r5)
    arrive(5, r5)
    pooled = total(r5, F).astype(BF16)
    row_part = dot(pooled, wo[...])
    for j in range(F):
        s6[j] = row_part[:, j * C:(j + 1) * C]
    scatter(6, s6, r6)
    class_raw = jnp.concatenate([r1[j][T:2 * T] for j in range(F)], axis=0)
    ld_wp.wait()
    arrive(6, r6)
    class_row = (class_raw + total(r6, F)).astype(BF16)
    s7[...] = stack_halves(dot(class_row, wp[...])).astype(BF16)
    spread(7, s7, r7)

    arrive_z(0, rm2)
    all_meta = total(rm2, S)
    all_order = all_meta[0:1, 0:N]
    all_present = all_meta[1:2, 0:N].astype(F32)
    position = lax.broadcasted_iota(jnp.int32, (N, N), 0) + 1
    picker = jnp.where(position == all_order, 1.0, 0.0)
    picker_tissue = (picker * all_present).astype(BF16)
    key_present = dot_t(jnp.broadcast_to(all_present, (8, N)).astype(BF16), picker.astype(BF16))[0:1]

    arrive(7, r7)
    s8[...] = total(r7, F).astype(BF16)
    spread_z(1, s8, r8)
    heads_dev = HC // (D // HEADS)
    hw = D // HEADS
    hr = (heads_dev, R, N)
    m_head = lax.broadcasted_iota(jnp.int32, hr, 0) + f * heads_dev
    m_row = lax.broadcasted_iota(jnp.int32, hr, 1) + z * R
    m_key = lax.broadcasted_iota(jnp.int32, hr, 2)
    segment = N // 4
    allowed = (key_present.reshape(1, 1, N) > 0.5) | (m_row == m_key)
    in_local = m_row // segment == m_key // segment
    in_dilated = (m_row % DILATION_STEP == m_head % DILATION_STEP) & (
        m_key % DILATION_STEP == m_head % DILATION_STEP)
    times = jnp.where(
        allowed, jnp.where(in_local, 1.0, 0.0) + jnp.where(in_dilated, 1.0, 0.0), 0.0
    ).reshape(heads_dev * R, N)
    a_head = lax.broadcasted_iota(jnp.int32, (heads_dev, R, HC), 0)
    a_col = lax.broadcasted_iota(jnp.int32, (heads_dev, R, HC), 2)
    mine = (a_col >= a_head * hw) & (a_col < (a_head + 1) * hw)
    ld_lq.wait()
    ld_lk.wait()
    ld_lv.wait()
    ld_lo.wait()
    arrive_z(1, r8)

    left = jnp.concatenate([r8[j].astype(F32)[:R] for j in range(S)], axis=0)
    right = jnp.concatenate([r8[j].astype(F32)[R:] for j in range(S)], axis=0)
    every = jnp.concatenate([left, right], axis=1).astype(BF16)
    sequence = dot(picker_tissue, every)
    lnormed = norm_rows(sequence, long_gain[...].reshape(1, D)).astype(BF16)
    qbuf[...] = dot_t(lnormed, lq[...])
    keys = dot_t(lnormed, lk[...]).astype(BF16)
    values = dot_t(lnormed, lv[...]).astype(BF16)
    queries = qbuf[pl.ds(pl.multiple_of(z * R, R), R), :].astype(BF16).astype(F32)
    per_head = jnp.where(mine, queries[None], 0.0).reshape(heads_dev * R, HC).astype(BF16)
    lifted = jnp.exp(dot_t(per_head, keys) / math.sqrt(hw))
    weights = lifted.astype(BF16).astype(F32) * times
    denominator = jnp.sum(lifted * times, axis=-1, keepdims=True)
    mixed = dot(weights.astype(BF16), values) / denominator
    attended = jnp.sum(
        jnp.where(mine, mixed.reshape(heads_dev, R, HC), 0.0), axis=0).astype(BF16)
    terms = dot(attended, lo[...])
    for j in range(F):
        s9[j] = terms[:, j * OC:(j + 1) * OC]
    scatter(8, s9, r9)
    for j in range(F):
        seqc[j] = sequence[:, j * OC:(j + 1) * OC]
    residual = seqc[f, pl.ds(pl.multiple_of(z * R, R), R), :]
    arrive(8, r9)
    out[...] = (residual + total(r9, F)).astype(BF16)
    for c in sends:
        c.wait_send()


def local(
    tile_patches, vit_gain, w_query, w_key, w_value, w_out, w_proj,
    long_gain, long_query, long_key, long_value, long_out, seq_order, counts,
):
    long_query, long_key, long_value = long_query.T, long_key.T, long_value.T
    S = lax.axis_size("seq")
    F = lax.axis_size("fsdp")
    T, PATCH, DV = tile_patches.shape
    VW = w_key.shape[1]
    D = w_proj.shape[1]
    R, C, HC, OC, PC = T * F, DV // F, long_query.shape[0], D // F, VW // F
    HP = up(VW // VHD, 16)
    N = R * S
    L = up(N, 128)
    V = pltpu.VMEM
    any_, vmem = pl.BlockSpec(memory_space=pl.ANY), pl.BlockSpec(memory_space=pltpu.VMEM)
    like = lambda a: V(a.shape, a.dtype)
    pair = lambda shape, dtype: [V((F,) + shape, dtype), V((F,) + shape, dtype)]
    fan = lambda n, shape, dtype: [V(shape, dtype), V((n,) + shape, dtype)]
    flops = 2 * (3 * R * HP * C * VW + 2 * T * HP * PATCH * DV + 3 * N * D * HC)
    return pl.pallas_call(
        functools.partial(kernel, F, S),
        out_shape=jax.ShapeDtypeStruct((R, OC), BF16),
        in_specs=[any_, vmem, any_, any_, any_, any_, any_, vmem,
                  any_, any_, any_, any_, any_, pl.BlockSpec(memory_space=pltpu.SMEM)],
        out_specs=vmem,
        scratch_shapes=[
            pltpu.SMEM(seq_order.shape, jnp.int32),
            V((T, 16, DV), BF16), like(tile_patches), V((T, F, PATCH, C), BF16),
            like(w_query), like(w_key), like(w_value), like(w_out), like(w_proj),
            like(long_query), like(long_key), like(long_value), like(long_out),
            *pair((up(2 * T, 8), C), F32),
            *fan(F, (8, L), jnp.int32),
            *fan(S, (8, L), jnp.int32),
            *fan(F, (2 * R, VW // 2), BF16),
            *pair((T * HP, C), BF16),
            *pair((T * HP, C), BF16),
            *pair((R, PC), F32),
            *pair((R, C), F32),
            *fan(F, (2 * R, D // 2), BF16),
            *fan(S, (2 * R, D // 2), BF16),
            *pair((R, OC), F32),
            V((N, HC), F32), V((F, N, OC), F32),
            pltpu.SemaphoreType.DMA((11 + T,)),
            pltpu.SemaphoreType.DMA((9, F)), pltpu.SemaphoreType.DMA((9, F)),
            pltpu.SemaphoreType.DMA((2, S)), pltpu.SemaphoreType.DMA((2, S)),
        ],
        compiler_params=pltpu.CompilerParams(
            collective_id=0, has_side_effects=True, vmem_limit_bytes=60 * 2**20),
        cost_estimate=pl.CostEstimate(
            flops=flops, bytes_accessed=8 * 2**20, transcendentals=T * HP * PATCH),
    )(
        tile_patches, vit_gain, w_query, w_key, w_value, w_out, w_proj,
        long_gain, long_query, long_key, long_value, long_out,
        seq_order, counts,
    )


def solution(mesh):
    return jax.shard_map(
        local,
        mesh=mesh,
        in_specs=(
            P(("group", "seq", "fsdp"), None, None),
            P(),
            P("fsdp", None),
            P("fsdp", None),
            P("fsdp", None),
            P("fsdp", None),
            P("fsdp", None),
            P(),
            P(None, "fsdp"),
            P(None, "fsdp"),
            P(None, "fsdp"),
            P("fsdp", None),
            P(("group", "seq", "fsdp")),
            P(("group", "seq", "fsdp")),
        ),
        out_specs=P(("group", "seq"), "fsdp"),
        check_vma=False,
    )
```

```python
import functools
import math

import jax
import jax.numpy as jnp
from jax import lax
from jax.experimental import pallas as pl
from jax.experimental.pallas import tpu as pltpu
from jax.sharding import PartitionSpec as P

VHD = 64
HEADS = 16
DILATION_STEP = 4
EPSILON = 1e-06
LN_ROWS = 64

F32 = jnp.float32
BF16 = jnp.bfloat16


def stack_halves(x):
    half = x.shape[1] // 2
    return jnp.concatenate([x[:, :half], x[:, half:]], axis=0)


def join_halves(x):
    half = x.shape[0] // 2
    return jnp.concatenate([x[:half], x[half:]], axis=1)


def up(n, m):
    return (n + m - 1) // m * m


def norm_rows(x, gain):
    mean = jnp.mean(x, axis=-1, keepdims=True)
    centred = x - mean
    variance = jnp.mean(centred * centred, axis=-1, keepdims=True)
    return centred * lax.rsqrt(variance + EPSILON) * gain


def dot(a, b):
    return jnp.dot(a, b, preferred_element_type=F32)


def dot_t(a, b):
    return lax.dot_general(a, b, (((1,), (1,)), ((), ())), preferred_element_type=F32)


def kernel(
    F, S,
    patches, vit_gain_hbm, w_query, w_key, w_value, w_out, w_proj,
    long_gain_hbm, long_query, long_key, long_value, long_out, order_hbm, counts,
    out, order, vit_gain, long_gain,
    cls, xbuf, normed, wq, wk, wv, wo, wp, lq, lk, lv, lo,
    s1, r1, sm, rm, sm2, rm2, s2, r2, s3, r3, s4, r4, s5, r5, s6, r6, s7, r7,
    s8, r8, s9, r9, qbuf, seqc,
    lsem, fsend, frecv, zsend, zrecv,
):
    T, PATCH, DV = patches.shape
    VW = w_key.shape[1]
    D = w_proj.shape[1]
    R = T * F
    N = R * S
    C = DV // F
    HC = long_query.shape[0]
    OC = D // F
    PC = VW // F
    HP = up(VW // VHD, 16)
    f = lax.axis_index("fsdp")
    z = lax.axis_index("seq")

    loads = []

    def load(src, dst):
        c = pltpu.make_async_copy(src, dst, lsem.at[len(loads)])
        c.start()
        loads.append(c)
        return c

    ld_cls = load(patches.at[:, pl.ds(0, 16), :], cls)
    ld_vg = load(vit_gain_hbm, vit_gain)
    barrier = pltpu.get_barrier_semaphore()
    for k in range(1, F):
        pl.semaphore_signal(
            barrier, inc=1, device_id={"fsdp": lax.rem(f + k, F)},
            device_id_type=pl.DeviceIdType.MESH)
    for k in range(1, S):
        pl.semaphore_signal(
            barrier, inc=1, device_id={"seq": lax.rem(z + k, S)},
            device_id_type=pl.DeviceIdType.MESH)
    ld_order = load(order_hbm, order)
    ld_wq = load(w_query, wq)
    ld_x = [load(patches.at[t], xbuf.at[t]) for t in range(T)]
    ld_wk = load(w_key, wk)
    ld_wv = load(w_value, wv)
    ld_wo = load(w_out, wo)
    ld_wp = load(w_proj, wp)
    ld_lg = load(long_gain_hbm, long_gain)
    ld_lq = load(long_query, lq)
    ld_lk = load(long_key, lk)
    ld_lv = load(long_value, lv)
    ld_lo = load(long_out, lo)

    sends = []

    def push(hop, axis, me, n, src, dst, send_sems, recv_sems):
        for k in sorted(range(1, n), key=lambda k: abs(2 * k - n)):
            peer = lax.rem(me + k, n)
            c = pltpu.make_async_remote_copy(
                src_ref=src(peer), dst_ref=dst.at[me],
                send_sem=send_sems.at[hop, k], recv_sem=recv_sems.at[hop, me],
                device_id={axis: peer}, device_id_type=pl.DeviceIdType.MESH)
            c.start()
            sends.append(c)

    def collect(hop, axis, me, n, dst, send_sems, recv_sems):
        for k in range(1, n):
            peer = lax.rem(me + k, n)
            pltpu.make_async_remote_copy(
                src_ref=dst.at[me], dst_ref=dst.at[peer],
                send_sem=send_sems.at[hop, k], recv_sem=recv_sems.at[hop, peer],
                device_id={axis: peer}, device_id_type=pl.DeviceIdType.MESH,
            ).wait_recv()

    def scatter(hop, src, dst):
        push(hop, "fsdp", f, F, lambda peer: src.at[peer], dst, fsend, frecv)
        dst[f] = src[f]

    def spread(hop, src, dst):
        push(hop, "fsdp", f, F, lambda peer: src, dst, fsend, frecv)
        dst[f] = src[...]

    def spread_z(hop, src, dst):
        push(hop, "seq", z, S, lambda peer: src, dst, zsend, zrecv)
        dst[z] = src[...]

    def arrive(hop, dst):
        collect(hop, "fsdp", f, F, dst, fsend, frecv)

    def arrive_z(hop, dst):
        collect(hop, "seq", z, S, dst, zsend, zrecv)

    def total(ref, n):
        part = lambda j: ref[j].astype(F32) if ref.dtype == BF16 else ref[j]
        acc = part(0)
        for j in range(1, n):
            acc = acc + part(j)
        return acc

    ld_cls.wait()
    ld_vg.wait()
    raw = jnp.concatenate([cls[t, 0:8, :].astype(F32)[0:1] for t in range(T)], axis=0)
    class_normed = norm_rows(raw, vit_gain[...].reshape(1, DV)).astype(BF16).astype(F32)
    filler = s1.shape[1] - 2 * T
    packed = jnp.concatenate(
        [class_normed, raw, jnp.zeros((filler, DV), F32)], axis=0)
    for j in range(F):
        s1[j] = packed[:, j * C:(j + 1) * C]
    pl.semaphore_wait(barrier, F - 1 + S - 1)
    scatter(0, s1, r1)
    ld_order.wait()
    L = sm.shape[1]
    lane = lax.broadcasted_iota(jnp.int32, sm.shape, 1)
    row = lax.broadcasted_iota(jnp.int32, sm.shape, 0)
    meta = jnp.zeros(sm.shape, jnp.int32)
    first = z * R + f * T
    for t in range(T):
        here = jnp.where(t < counts[0], 1, 0)
        value = jnp.where(row == 0, order[t] + 1, jnp.where(row == 1, here, 0))
        meta = jnp.where(lane == first + t, value, meta)
    sm[...] = meta
    spread(1, sm, rm)

    blocks = PATCH // LN_ROWS

    def norm_blocks(lo_block, hi_block):
        def body(i, carry):
            t = i // blocks
            start = pl.multiple_of((i % blocks) * LN_ROWS, LN_ROWS)
            x = xbuf[t, pl.ds(start, LN_ROWS), :].astype(F32)
            y = norm_rows(x, vit_gain[...].reshape(1, DV))
            for j in range(F):
                normed[t, j, pl.ds(start, LN_ROWS), :] = y[:, j * C:(j + 1) * C].astype(BF16)
            return carry
        lax.fori_loop(lo_block, hi_block, body, 0)

    cuts = (3 * T * blocks // 8, 5 * T * blocks // 8)
    for c in ld_x:
        c.wait()
    norm_blocks(0, cuts[0])

    ld_wq.wait()
    arrive(0, r1)
    xq = jnp.concatenate([r1[j][0:T] for j in range(F)], axis=0)
    s2[...] = stack_halves(dot(xq.astype(BF16), wq[...])).astype(BF16)
    spread(2, s2, r2)
    arrive(1, rm)
    sm2[...] = total(rm, F)
    spread_z(0, sm2, rm2)
    norm_blocks(*cuts)
    head = lax.broadcasted_iota(jnp.int32, (R, HP, VW), 1)
    column = lax.broadcasted_iota(jnp.int32, (R, HP, VW), 2)
    own_head = (column >= head * VHD) & (column < (head + 1) * VHD)
    ld_wk.wait()
    arrive(2, r2)
    query = join_halves(total(r2, F).astype(BF16).astype(F32))

    spread_query = jnp.where(own_head, query[:, None, :], 0.0).reshape(R * HP, VW)
    folded = dot_t(spread_query.astype(BF16), wk[...]).astype(BF16)
    s3[...] = folded.reshape(F, T * HP, C)
    scatter(3, s3, r3)
    norm_blocks(cuts[1], T * blocks)
    arrive(3, r3)

    for t in range(T):
        scores = dot_t(r3[0, pl.ds(t * HP, HP), :], normed[t, 0])
        for j in range(1, F):
            scores = scores + dot_t(r3[j, pl.ds(t * HP, HP), :], normed[t, j])
        lifted = jnp.exp(scores / math.sqrt(VHD))
        probs = (lifted / jnp.sum(lifted, axis=-1, keepdims=True)).astype(BF16)
        for j in range(F):
            s4[j, pl.ds(t * HP, HP), :] = dot(probs, normed[t, j]).astype(BF16)
    scatter(4, s4, r4)
    ld_wv.wait()
    ld_wo.wait()
    arrive(4, r4)

    summed = dot(r4[...].reshape(R * HP, C), wv[...]).reshape(R, HP, VW)
    pooled_part = jnp.sum(jnp.where(own_head, summed, 0.0), axis=1)
    for j in range(F):
        s5[j] = pooled_part[:, j * PC:(j + 1) * PC]
    scatter(5, s5, r5)
    heads_dev = HC // (D // HEADS)
    hw = D // HEADS
    hr = (heads_dev, R, N)
    m_head = lax.broadcasted_iota(jnp.int32, hr, 0) + f * heads_dev
    m_row = lax.broadcasted_iota(jnp.int32, hr, 1) + z * R
    m_key = lax.broadcasted_iota(jnp.int32, hr, 2)
    segment = N // 4
    in_local = m_row // segment == m_key // segment
    in_dilated = (m_row % DILATION_STEP == m_head % DILATION_STEP) & (
        m_key % DILATION_STEP == m_head % DILATION_STEP)
    sets = jnp.where(in_local, 1.0, 0.0) + jnp.where(in_dilated, 1.0, 0.0)
    a_head = lax.broadcasted_iota(jnp.int32, (heads_dev, R, HC), 0)
    a_col = lax.broadcasted_iota(jnp.int32, (heads_dev, R, HC), 2)
    mine = (a_col >= a_head * hw) & (a_col < (a_head + 1) * hw)
    arrive(5, r5)
    pooled = total(r5, F).astype(BF16)
    row_part = dot(pooled, wo[...])
    for j in range(F):
        s6[j] = row_part[:, j * C:(j + 1) * C]
    scatter(6, s6, r6)
    class_raw = jnp.concatenate([r1[j][T:2 * T] for j in range(F)], axis=0)
    ld_wp.wait()
    arrive(6, r6)
    class_row = (class_raw + total(r6, F)).astype(BF16)
    s7[...] = stack_halves(dot(class_row, wp[...])).astype(BF16)
    spread(7, s7, r7)

    arrive_z(0, rm2)
    all_meta = total(rm2, S)
    all_order = all_meta[0:1, 0:N]
    all_present = all_meta[1:2, 0:N].astype(F32)
    position = lax.broadcasted_iota(jnp.int32, (N, N), 0) + 1
    picker = jnp.where(position == all_order, 1.0, 0.0)
    picker_tissue = (picker * all_present).astype(BF16)
    key_present = dot_t(jnp.broadcast_to(all_present, (8, N)).astype(BF16), picker.astype(BF16))[0:1]

    allowed = (key_present.reshape(1, 1, N) > 0.5) | (m_row == m_key)
    times = jnp.where(allowed, sets, 0.0).reshape(heads_dev * R, N)
    arrive(7, r7)
    s8[...] = total(r7, F).astype(BF16)
    spread_z(1, s8, r8)
    ld_lg.wait()
    ld_lq.wait()
    ld_lk.wait()
    ld_lv.wait()
    ld_lo.wait()
    arrive_z(1, r8)

    left = jnp.concatenate([r8[j].astype(F32)[:R] for j in range(S)], axis=0)
    right = jnp.concatenate([r8[j].astype(F32)[R:] for j in range(S)], axis=0)
    every = jnp.concatenate([left, right], axis=1).astype(BF16)
    sequence = dot(picker_tissue, every)
    lnormed = norm_rows(sequence, long_gain[...].reshape(1, D)).astype(BF16)
    qbuf[...] = dot_t(lnormed, lq[...])
    keys = dot_t(lnormed, lk[...]).astype(BF16)
    values = dot_t(lnormed, lv[...]).astype(BF16)
    queries = qbuf[pl.ds(pl.multiple_of(z * R, R), R), :].astype(BF16).astype(F32)
    per_head = jnp.where(mine, queries[None], 0.0).reshape(heads_dev * R, HC).astype(BF16)
    lifted = jnp.exp(dot_t(per_head, keys) / math.sqrt(hw))
    weights = lifted.astype(BF16).astype(F32) * times
    denominator = jnp.sum(lifted * times, axis=-1, keepdims=True)
    mixed = dot(weights.astype(BF16), values) / denominator
    attended = jnp.sum(
        jnp.where(mine, mixed.reshape(heads_dev, R, HC), 0.0), axis=0).astype(BF16)
    terms = dot(attended, lo[...])
    for j in range(F):
        s9[j] = terms[:, j * OC:(j + 1) * OC]
    scatter(8, s9, r9)
    for j in range(F):
        seqc[j] = sequence[:, j * OC:(j + 1) * OC]
    residual = seqc[f, pl.ds(pl.multiple_of(z * R, R), R), :]
    arrive(8, r9)
    out[...] = (residual + total(r9, F)).astype(BF16)
    for c in sends:
        c.wait_send()


def local(
    tile_patches, vit_gain, w_query, w_key, w_value, w_out, w_proj,
    long_gain, long_query, long_key, long_value, long_out, seq_order, counts,
):
    long_query, long_key, long_value = long_query.T, long_key.T, long_value.T
    S = lax.axis_size("seq")
    F = lax.axis_size("fsdp")
    T, PATCH, DV = tile_patches.shape
    VW = w_key.shape[1]
    D = w_proj.shape[1]
    R, C, HC, OC, PC = T * F, DV // F, long_query.shape[0], D // F, VW // F
    HP = up(VW // VHD, 16)
    N = R * S
    L = up(N, 128)
    V = pltpu.VMEM
    any_, vmem = pl.BlockSpec(memory_space=pl.ANY), pl.BlockSpec(memory_space=pltpu.VMEM)
    like = lambda a: V(a.shape, a.dtype)
    pair = lambda shape, dtype: [V((F,) + shape, dtype), V((F,) + shape, dtype)]
    fan = lambda n, shape, dtype: [V(shape, dtype), V((n,) + shape, dtype)]
    flops = 2 * (3 * R * HP * C * VW + 2 * T * HP * PATCH * DV + 3 * N * D * HC)
    return pl.pallas_call(
        functools.partial(kernel, F, S),
        out_shape=pltpu.VMEM((R, OC), BF16),
        in_specs=[any_, any_, any_, any_, any_, any_, any_, any_,
                  any_, any_, any_, any_, any_, pl.BlockSpec(memory_space=pltpu.SMEM)],
        out_specs=vmem,
        scratch_shapes=[
            pltpu.SMEM(seq_order.shape, jnp.int32), like(vit_gain), like(long_gain),
            V((T, 16, DV), BF16), like(tile_patches), V((T, F, PATCH, C), BF16),
            like(w_query), like(w_key), like(w_value), like(w_out), like(w_proj),
            like(long_query), like(long_key), like(long_value), like(long_out),
            *pair((up(2 * T, 8), C), F32),
            *fan(F, (8, L), jnp.int32),
            *fan(S, (8, L), jnp.int32),
            *fan(F, (2 * R, VW // 2), BF16),
            *pair((T * HP, C), BF16),
            *pair((T * HP, C), BF16),
            *pair((R, PC), F32),
            *pair((R, C), F32),
            *fan(F, (2 * R, D // 2), BF16),
            *fan(S, (2 * R, D // 2), BF16),
            *pair((R, OC), F32),
            V((N, HC), F32), V((F, N, OC), F32),
            pltpu.SemaphoreType.DMA((13 + T,)),
            pltpu.SemaphoreType.DMA((9, F)), pltpu.SemaphoreType.DMA((9, F)),
            pltpu.SemaphoreType.DMA((2, S)), pltpu.SemaphoreType.DMA((2, S)),
        ],
        compiler_params=pltpu.CompilerParams(
            collective_id=0, has_side_effects=True, vmem_limit_bytes=60 * 2**20),
        cost_estimate=pl.CostEstimate(
            flops=flops, bytes_accessed=8 * 2**20, transcendentals=T * HP * PATCH),
    )(
        tile_patches, vit_gain, w_query, w_key, w_value, w_out, w_proj,
        long_gain, long_query, long_key, long_value, long_out,
        seq_order, counts,
    )


def solution(mesh):
    return jax.shard_map(
        local,
        mesh=mesh,
        in_specs=(
            P(("group", "seq", "fsdp"), None, None),
            P(),
            P("fsdp", None),
            P("fsdp", None),
            P("fsdp", None),
            P("fsdp", None),
            P("fsdp", None),
            P(),
            P(None, "fsdp"),
            P(None, "fsdp"),
            P(None, "fsdp"),
            P("fsdp", None),
            P(("group", "seq", "fsdp")),
            P(("group", "seq", "fsdp")),
        ),
        out_specs=P(("group", "seq"), "fsdp"),
        check_vma=False,
    )
```

```python
import functools
import math

import jax
import jax.numpy as jnp
from jax import lax
from jax.experimental import pallas as pl
from jax.experimental.pallas import tpu as pltpu
from jax.sharding import PartitionSpec as P

VHD = 64
HEADS = 16
DILATION_STEP = 4
EPSILON = 1e-06
LN_ROWS = 64

F32 = jnp.float32
BF16 = jnp.bfloat16


def stack_halves(x):
    half = x.shape[1] // 2
    return jnp.concatenate([x[:, :half], x[:, half:]], axis=0)


def join_halves(x):
    half = x.shape[0] // 2
    return jnp.concatenate([x[:half], x[half:]], axis=1)


def up(n, m):
    return (n + m - 1) // m * m


def norm_rows(x, gain):
    mean = jnp.mean(x, axis=-1, keepdims=True)
    centred = x - mean
    variance = jnp.mean(centred * centred, axis=-1, keepdims=True)
    return centred * lax.rsqrt(variance + EPSILON) * gain


def dot(a, b):
    return jnp.dot(a, b, preferred_element_type=F32)


def dot_t(a, b):
    return lax.dot_general(a, b, (((1,), (1,)), ((), ())), preferred_element_type=F32)


def kernel(
    F, S,
    patches, vit_gain_hbm, w_query, w_key, w_value, w_out, w_proj,
    long_gain_hbm, long_query, long_key, long_value, long_out, order_hbm, counts,
    out, order, vit_gain, long_gain,
    cls, xbuf, normed, wq, wk, wv, wo, wp, lq, lk, lv, lo,
    s1, r1, sm, rm, sm2, rm2, s2, r2, s3, r3, s4, r4, s5, r5, s6, r6, s7, r7,
    s8, r8, s9, r9, qbuf, seqc,
    lsem, fsend, frecv, zsend, zrecv,
):
    T, PATCH, DV = patches.shape
    VW = w_key.shape[1]
    D = w_proj.shape[1]
    R = T * F
    N = R * S
    C = DV // F
    HC = long_query.shape[0]
    OC = D // F
    PC = VW // F
    HP = up(VW // VHD, 16)
    f = lax.axis_index("fsdp")
    z = lax.axis_index("seq")

    loads = []

    def load(src, dst):
        c = pltpu.make_async_copy(src, dst, lsem.at[len(loads)])
        c.start()
        loads.append(c)
        return c

    ld_cls = load(patches.at[:, pl.ds(0, 16), :], cls)
    ld_vg = load(vit_gain_hbm, vit_gain)
    barrier = pltpu.get_barrier_semaphore()
    for k in range(1, F):
        pl.semaphore_signal(
            barrier, inc=1, device_id={"fsdp": lax.rem(f + k, F)},
            device_id_type=pl.DeviceIdType.MESH)
    for k in range(1, S):
        pl.semaphore_signal(
            barrier, inc=1, device_id={"seq": lax.rem(z + k, S)},
            device_id_type=pl.DeviceIdType.MESH)
    ld_order = load(order_hbm, order)
    ld_wq = load(w_query, wq)
    ld_x = [load(patches.at[t], xbuf.at[t]) for t in range(T)]
    ld_wk = load(w_key, wk)
    ld_wv = load(w_value, wv)
    ld_wo = load(w_out, wo)
    ld_wp = load(w_proj, wp)
    ld_lg = load(long_gain_hbm, long_gain)
    ld_lq = load(long_query, lq)
    ld_lk = load(long_key, lk)
    ld_lv = load(long_value, lv)
    ld_lo = load(long_out, lo)

    sends = []

    def push(hop, axis, me, n, src, dst, send_sems, recv_sems):
        for k in sorted(range(1, n), key=lambda k: abs(2 * k - n)):
            peer = lax.rem(me + k, n)
            c = pltpu.make_async_remote_copy(
                src_ref=src(peer), dst_ref=dst.at[me],
                send_sem=send_sems.at[hop, k], recv_sem=recv_sems.at[hop, me],
                device_id={axis: peer}, device_id_type=pl.DeviceIdType.MESH)
            c.start()
            sends.append(c)

    def collect(hop, axis, me, n, dst, send_sems, recv_sems):
        for k in range(1, n):
            peer = lax.rem(me + k, n)
            pltpu.make_async_remote_copy(
                src_ref=dst.at[me], dst_ref=dst.at[peer],
                send_sem=send_sems.at[hop, k], recv_sem=recv_sems.at[hop, peer],
                device_id={axis: peer}, device_id_type=pl.DeviceIdType.MESH,
            ).wait_recv()

    def scatter(hop, src, dst):
        push(hop, "fsdp", f, F, lambda peer: src.at[peer], dst, fsend, frecv)
        dst[f] = src[f]

    def spread(hop, src, dst):
        push(hop, "fsdp", f, F, lambda peer: src, dst, fsend, frecv)
        dst[f] = src[...]

    def spread_z(hop, src, dst):
        push(hop, "seq", z, S, lambda peer: src, dst, zsend, zrecv)
        dst[z] = src[...]

    def arrive(hop, dst):
        collect(hop, "fsdp", f, F, dst, fsend, frecv)

    def arrive_z(hop, dst):
        collect(hop, "seq", z, S, dst, zsend, zrecv)

    def total(ref, n):
        part = lambda j: ref[j].astype(F32) if ref.dtype == BF16 else ref[j]
        acc = part(0)
        for j in range(1, n):
            acc = acc + part(j)
        return acc

    ld_cls.wait()
    ld_vg.wait()
    raw = jnp.concatenate([cls[t, 0:8, :].astype(F32)[0:1] for t in range(T)], axis=0)
    class_normed = norm_rows(raw, vit_gain[...].reshape(1, DV)).astype(BF16).astype(F32)
    filler = s1.shape[1] - 2 * T
    packed = jnp.concatenate(
        [class_normed, raw, jnp.zeros((filler, DV), F32)], axis=0)
    for j in range(F):
        s1[j] = packed[:, j * C:(j + 1) * C]
    pl.semaphore_wait(barrier, F - 1 + S - 1)
    scatter(0, s1, r1)
    ld_order.wait()
    L = sm.shape[1]
    lane = lax.broadcasted_iota(jnp.int32, sm.shape, 1)
    row = lax.broadcasted_iota(jnp.int32, sm.shape, 0)
    meta = jnp.zeros(sm.shape, jnp.int32)
    first = z * R + f * T
    for t in range(T):
        here = jnp.where(t < counts[0], 1, 0)
        value = jnp.where(row == 0, order[t] + 1, jnp.where(row == 1, here, 0))
        meta = jnp.where(lane == first + t, value, meta)
    sm[...] = meta
    spread(1, sm, rm)

    blocks = PATCH // LN_ROWS

    def norm_blocks(lo_block, hi_block):
        def body(i, carry):
            t = i // blocks
            start = pl.multiple_of((i % blocks) * LN_ROWS, LN_ROWS)
            x = xbuf[t, pl.ds(start, LN_ROWS), :].astype(F32)
            y = norm_rows(x, vit_gain[...].reshape(1, DV))
            for j in range(F):
                normed[t, j, pl.ds(start, LN_ROWS), :] = y[:, j * C:(j + 1) * C].astype(BF16)
            return carry
        lax.fori_loop(lo_block, hi_block, body, 0)

    cuts = (3 * T * blocks // 8, 5 * T * blocks // 8)
    for c in ld_x:
        c.wait()
    norm_blocks(0, cuts[0])

    ld_wq.wait()
    arrive(0, r1)
    xq = jnp.concatenate([r1[j][0:T] for j in range(F)], axis=0)
    s2[...] = stack_halves(dot(xq.astype(BF16), wq[...])).astype(BF16)
    spread(2, s2, r2)
    arrive(1, rm)
    sm2[...] = total(rm, F)
    spread_z(0, sm2, rm2)
    norm_blocks(*cuts)
    head = lax.broadcasted_iota(jnp.int32, (R, HP, VW), 1)
    column = lax.broadcasted_iota(jnp.int32, (R, HP, VW), 2)
    own_head = (column >= head * VHD) & (column < (head + 1) * VHD)
    ld_wk.wait()
    arrive(2, r2)
    query = join_halves(total(r2, F).astype(BF16).astype(F32))

    spread_query = jnp.where(own_head, query[:, None, :], 0.0).reshape(R * HP, VW)
    folded = dot_t(spread_query.astype(BF16), wk[...]).astype(BF16)
    s3[...] = folded.reshape(F, T * HP, C)
    scatter(3, s3, r3)
    norm_blocks(cuts[1], T * blocks)
    arrive(3, r3)

    for t in range(T):
        by_token = dot_t(normed[t, 0], r3[0])
        for j in range(1, F):
            by_token = by_token + dot_t(normed[t, j], r3[j])
        scores = jnp.transpose(by_token)[t * HP:(t + 1) * HP]
        lifted = jnp.exp(scores / math.sqrt(VHD))
        probs = (lifted / jnp.sum(lifted, axis=-1, keepdims=True)).astype(BF16)
        for j in range(F):
            s4[j, pl.ds(t * HP, HP), :] = dot(probs, normed[t, j]).astype(BF16)
    scatter(4, s4, r4)
    ld_wv.wait()
    ld_wo.wait()
    arrive(4, r4)

    summed = dot(r4[...].reshape(R * HP, C), wv[...]).reshape(R, HP, VW)
    pooled_part = jnp.sum(jnp.where(own_head, summed, 0.0), axis=1)
    for j in range(F):
        s5[j] = pooled_part[:, j * PC:(j + 1) * PC]
    scatter(5, s5, r5)
    heads_dev = HC // (D // HEADS)
    hw = D // HEADS
    hr = (heads_dev, R, N)
    m_head = lax.broadcasted_iota(jnp.int32, hr, 0) + f * heads_dev
    m_row = lax.broadcasted_iota(jnp.int32, hr, 1) + z * R
    m_key = lax.broadcasted_iota(jnp.int32, hr, 2)
    segment = N // 4
    in_local = m_row // segment == m_key // segment
    in_dilated = (m_row % DILATION_STEP == m_head % DILATION_STEP) & (
        m_key % DILATION_STEP == m_head % DILATION_STEP)
    sets = jnp.where(in_local, 1.0, 0.0) + jnp.where(in_dilated, 1.0, 0.0)
    a_head = lax.broadcasted_iota(jnp.int32, (heads_dev, R, HC), 0)
    a_col = lax.broadcasted_iota(jnp.int32, (heads_dev, R, HC), 2)
    mine = (a_col >= a_head * hw) & (a_col < (a_head + 1) * hw)
    arrive(5, r5)
    pooled = total(r5, F).astype(BF16)
    row_part = dot(pooled, wo[...])
    for j in range(F):
        s6[j] = row_part[:, j * C:(j + 1) * C]
    scatter(6, s6, r6)
    class_raw = jnp.concatenate([r1[j][T:2 * T] for j in range(F)], axis=0)
    ld_wp.wait()
    arrive(6, r6)
    class_row = (class_raw + total(r6, F)).astype(BF16)
    s7[...] = stack_halves(dot(class_row, wp[...])).astype(BF16)
    spread(7, s7, r7)

    arrive_z(0, rm2)
    all_meta = total(rm2, S)
    all_order = all_meta[0:1, 0:N]
    all_present = all_meta[1:2, 0:N].astype(F32)
    position = lax.broadcasted_iota(jnp.int32, (N, N), 0) + 1
    picker = jnp.where(position == all_order, 1.0, 0.0)
    picker_tissue = (picker * all_present).astype(BF16)
    key_present = dot_t(jnp.broadcast_to(all_present, (8, N)).astype(BF16), picker.astype(BF16))[0:1]

    allowed = (key_present.reshape(1, 1, N) > 0.5) | (m_row == m_key)
    times = jnp.where(allowed, sets, 0.0).reshape(heads_dev * R, N)
    arrive(7, r7)
    s8[...] = total(r7, F).astype(BF16)
    spread_z(1, s8, r8)
    ld_lg.wait()
    ld_lq.wait()
    ld_lk.wait()
    ld_lv.wait()
    ld_lo.wait()
    arrive_z(1, r8)

    left = jnp.concatenate([r8[j].astype(F32)[:R] for j in range(S)], axis=0)
    right = jnp.concatenate([r8[j].astype(F32)[R:] for j in range(S)], axis=0)
    every = jnp.concatenate([left, right], axis=1).astype(BF16)
    sequence = dot(picker_tissue, every)
    lnormed = norm_rows(sequence, long_gain[...].reshape(1, D)).astype(BF16)
    qbuf[...] = dot_t(lnormed, lq[...])
    keys = dot_t(lnormed, lk[...]).astype(BF16)
    values = dot_t(lnormed, lv[...]).astype(BF16)
    queries = qbuf[pl.ds(pl.multiple_of(z * R, R), R), :].astype(BF16).astype(F32)
    per_head = jnp.where(mine, queries[None], 0.0).reshape(heads_dev * R, HC).astype(BF16)
    lifted = jnp.exp(dot_t(per_head, keys) / math.sqrt(hw))
    weights = lifted.astype(BF16).astype(F32) * times
    denominator = jnp.sum(lifted * times, axis=-1, keepdims=True)
    mixed = dot(weights.astype(BF16), values) / denominator
    attended = jnp.sum(
        jnp.where(mine, mixed.reshape(heads_dev, R, HC), 0.0), axis=0).astype(BF16)
    terms = dot(attended, lo[...])
    for j in range(F):
        s9[j] = terms[:, j * OC:(j + 1) * OC]
    scatter(8, s9, r9)
    for j in range(F):
        seqc[j] = sequence[:, j * OC:(j + 1) * OC]
    residual = seqc[f, pl.ds(pl.multiple_of(z * R, R), R), :]
    for c in sends[:1 - F]:
        c.wait_send()
    arrive(8, r9)
    out[...] = (residual + total(r9, F)).astype(BF16)
    for c in sends[1 - F:]:
        c.wait_send()


def local(
    tile_patches, vit_gain, w_query, w_key, w_value, w_out, w_proj,
    long_gain, long_query, long_key, long_value, long_out, seq_order, counts,
):
    long_query, long_key, long_value = long_query.T, long_key.T, long_value.T
    S = lax.axis_size("seq")
    F = lax.axis_size("fsdp")
    T, PATCH, DV = tile_patches.shape
    VW = w_key.shape[1]
    D = w_proj.shape[1]
    R, C, HC, OC, PC = T * F, DV // F, long_query.shape[0], D // F, VW // F
    HP = up(VW // VHD, 16)
    N = R * S
    L = up(N, 128)
    V = pltpu.VMEM
    any_, vmem = pl.BlockSpec(memory_space=pl.ANY), pl.BlockSpec(memory_space=pltpu.VMEM)
    like = lambda a: V(a.shape, a.dtype)
    pair = lambda shape, dtype: [V((F,) + shape, dtype), V((F,) + shape, dtype)]
    fan = lambda n, shape, dtype: [V(shape, dtype), V((n,) + shape, dtype)]
    flops = 2 * (3 * R * HP * C * VW + 2 * T * HP * PATCH * DV + 3 * N * D * HC)
    return pl.pallas_call(
        functools.partial(kernel, F, S),
        out_shape=pltpu.VMEM((R, OC), BF16),
        in_specs=[any_, any_, any_, any_, any_, any_, any_, any_,
                  any_, any_, any_, any_, any_, pl.BlockSpec(memory_space=pltpu.SMEM)],
        out_specs=vmem,
        scratch_shapes=[
            pltpu.SMEM(seq_order.shape, jnp.int32), like(vit_gain), like(long_gain),
            V((T, 16, DV), BF16), like(tile_patches), V((T, F, PATCH, C), BF16),
            like(w_query), like(w_key), like(w_value), like(w_out), like(w_proj),
            like(long_query), like(long_key), like(long_value), like(long_out),
            *pair((up(2 * T, 8), C), F32),
            *fan(F, (8, L), jnp.int32),
            *fan(S, (8, L), jnp.int32),
            *fan(F, (2 * R, VW // 2), BF16),
            *pair((T * HP, C), BF16),
            *pair((T * HP, C), BF16),
            *pair((R, PC), F32),
            *pair((R, C), F32),
            *fan(F, (2 * R, D // 2), BF16),
            *fan(S, (2 * R, D // 2), BF16),
            *pair((R, OC), F32),
            V((N, HC), F32), V((F, N, OC), F32),
            pltpu.SemaphoreType.DMA((13 + T,)),
            pltpu.SemaphoreType.DMA((9, F)), pltpu.SemaphoreType.DMA((9, F)),
            pltpu.SemaphoreType.DMA((2, S)), pltpu.SemaphoreType.DMA((2, S)),
        ],
        compiler_params=pltpu.CompilerParams(
            collective_id=0, has_side_effects=True, vmem_limit_bytes=60 * 2**20),
        cost_estimate=pl.CostEstimate(
            flops=flops, bytes_accessed=8 * 2**20, transcendentals=T * HP * PATCH),
    )(
        tile_patches, vit_gain, w_query, w_key, w_value, w_out, w_proj,
        long_gain, long_query, long_key, long_value, long_out,
        seq_order, counts,
    )


def solution(mesh):
    return jax.shard_map(
        local,
        mesh=mesh,
        in_specs=(
            P(("group", "seq", "fsdp"), None, None),
            P(),
            P("fsdp", None),
            P("fsdp", None),
            P("fsdp", None),
            P("fsdp", None),
            P("fsdp", None),
            P(),
            P(None, "fsdp"),
            P(None, "fsdp"),
            P(None, "fsdp"),
            P("fsdp", None),
            P(("group", "seq", "fsdp")),
            P(("group", "seq", "fsdp")),
        ),
        out_specs=P(("group", "seq"), "fsdp"),
        check_vma=False,
    )
```

```python
import functools
import math

import jax
import jax.numpy as jnp
from jax import lax
from jax.experimental import pallas as pl
from jax.experimental.pallas import tpu as pltpu
from jax.sharding import PartitionSpec as P

VHD = 64
HEADS = 16
DILATION_STEP = 4
EPSILON = 1e-06
LN_ROWS = 64

F32 = jnp.float32
BF16 = jnp.bfloat16


def stack_halves(x):
    half = x.shape[1] // 2
    return jnp.concatenate([x[:, :half], x[:, half:]], axis=0)


def join_halves(x):
    half = x.shape[0] // 2
    return jnp.concatenate([x[:half], x[half:]], axis=1)


def up(n, m):
    return (n + m - 1) // m * m


def partners(me, n):
    if n % 2:
        return [lax.rem(me + k, n) for k in range(1, n)]
    pair, side = me // 2, me % 2
    found = []
    for k in range(1, n // 2):
        other = lax.rem(pair + k, n // 2) * 2
        found += [other + side, other + 1 - side]
    return found + [pair * 2 + 1 - side]


def norm_rows(x, gain):
    mean = jnp.mean(x, axis=-1, keepdims=True)
    centred = x - mean
    variance = jnp.mean(centred * centred, axis=-1, keepdims=True)
    return centred * lax.rsqrt(variance + EPSILON) * gain


def dot(a, b):
    return jnp.dot(a, b, preferred_element_type=F32)


def dot_t(a, b):
    return lax.dot_general(a, b, (((1,), (1,)), ((), ())), preferred_element_type=F32)


def kernel(
    F, S,
    patches, vit_gain_hbm, w_query, w_key, w_value, w_out, w_proj,
    long_gain_hbm, long_query, long_key, long_value, long_out, order_hbm, counts,
    out, order, vit_gain, long_gain,
    cls, xbuf, normed, wq, wk, wv, wo, wp, lqkv, lo,
    s1, r1, sm, rm, sm2, rm2, s2, r2, s3, r3, s4, r4, s5, r5, s6, r6, s7, r7,
    s8, r8, s9, r9, qbuf, seqc,
    lsem, fsend, frecv, zsend, zrecv,
):
    T, PATCH, DV = patches.shape
    VW = w_key.shape[1]
    D = w_proj.shape[1]
    R = T * F
    N = R * S
    C = DV // F
    HC = long_query.shape[0]
    OC = D // F
    PC = VW // F
    HP = up(VW // VHD, 16)
    f = lax.axis_index("fsdp")
    z = lax.axis_index("seq")

    loads = []

    def load(src, dst):
        c = pltpu.make_async_copy(src, dst, lsem.at[len(loads)])
        c.start()
        loads.append(c)
        return c

    ld_cls = load(patches.at[:, pl.ds(0, 16), :], cls)
    ld_vg = load(vit_gain_hbm, vit_gain)
    barrier = pltpu.get_barrier_semaphore()
    for k in range(1, F):
        pl.semaphore_signal(
            barrier, inc=1, device_id={"fsdp": lax.rem(f + k, F)},
            device_id_type=pl.DeviceIdType.MESH)
    for k in range(1, S):
        pl.semaphore_signal(
            barrier, inc=1, device_id={"seq": lax.rem(z + k, S)},
            device_id_type=pl.DeviceIdType.MESH)
    ld_order = load(order_hbm, order)
    ld_wq = load(w_query, wq)
    ld_x = [load(patches.at[t], xbuf.at[t]) for t in range(T)]
    ld_wk = load(w_key, wk)
    ld_wv = load(w_value, wv)
    ld_wo = load(w_out, wo)
    ld_wp = load(w_proj, wp)
    ld_lg = load(long_gain_hbm, long_gain)
    ld_lq = load(long_query, lqkv.at[0])
    ld_lk = load(long_key, lqkv.at[1])
    ld_lv = load(long_value, lqkv.at[2])
    ld_lo = load(long_out, lo)

    sends = []

    def push(hop, axis, me, n, src, dst, send_sems, recv_sems):
        for k, peer in enumerate(partners(me, n)):
            c = pltpu.make_async_remote_copy(
                src_ref=src(peer), dst_ref=dst.at[me],
                send_sem=send_sems.at[hop, k], recv_sem=recv_sems.at[hop, me],
                device_id={axis: peer}, device_id_type=pl.DeviceIdType.MESH)
            c.start()
            sends.append(c)

    def collect(hop, axis, me, n, dst, send_sems, recv_sems):
        for k, peer in enumerate(reversed(partners(me, n))):
            pltpu.make_async_remote_copy(
                src_ref=dst.at[me], dst_ref=dst.at[peer],
                send_sem=send_sems.at[hop, k], recv_sem=recv_sems.at[hop, peer],
                device_id={axis: peer}, device_id_type=pl.DeviceIdType.MESH,
            ).wait_recv()

    def scatter(hop, src, dst):
        push(hop, "fsdp", f, F, lambda peer: src.at[peer], dst, fsend, frecv)
        dst[f] = src[f]

    def spread(hop, src, dst):
        push(hop, "fsdp", f, F, lambda peer: src, dst, fsend, frecv)
        dst[f] = src[...]

    def spread_z(hop, src, dst):
        push(hop, "seq", z, S, lambda peer: src, dst, zsend, zrecv)
        dst[z] = src[...]

    def arrive(hop, dst):
        collect(hop, "fsdp", f, F, dst, fsend, frecv)

    def arrive_z(hop, dst):
        collect(hop, "seq", z, S, dst, zsend, zrecv)

    def total(ref, n):
        part = lambda j: ref[j].astype(F32) if ref.dtype == BF16 else ref[j]
        acc = part(0)
        for j in range(1, n):
            acc = acc + part(j)
        return acc

    ld_cls.wait()
    ld_vg.wait()
    raw = jnp.concatenate([cls[t, 0:8, :].astype(F32)[0:1] for t in range(T)], axis=0)
    class_normed = norm_rows(raw, vit_gain[...].reshape(1, DV)).astype(BF16).astype(F32)
    filler = s1.shape[1] - 2 * T
    packed = jnp.concatenate(
        [class_normed, raw, jnp.zeros((filler, DV), F32)], axis=0)
    for j in range(F):
        s1[j] = packed[:, j * C:(j + 1) * C]
    pl.semaphore_wait(barrier, F - 1 + S - 1)
    scatter(0, s1, r1)
    ld_order.wait()
    L = sm.shape[1]
    lane = lax.broadcasted_iota(jnp.int32, sm.shape, 1)
    row = lax.broadcasted_iota(jnp.int32, sm.shape, 0)
    meta = jnp.zeros(sm.shape, jnp.int32)
    first = z * R + f * T
    for t in range(T):
        here = jnp.where(t < counts[0], 1, 0)
        value = jnp.where(row == 0, order[t] + 1, jnp.where(row == 1, here, 0))
        meta = jnp.where(lane == first + t, value, meta)
        split = 2 * z * R + f * T + t + jnp.where(row == 3, R, 0)
        meta = jnp.where(
            (row >= 2) & (row < 4) & (lane == split), jnp.where(t < counts[0], order[t] + 1, 0), meta)
    sm[...] = meta
    spread(1, sm, rm)

    s5[...] = jnp.zeros(s5.shape, F32)
    s9[...] = jnp.zeros(s9.shape, F32)
    blocks = PATCH // LN_ROWS

    def norm_blocks(lo_block, hi_block):
        def body(i, carry):
            t = i // blocks
            start = pl.multiple_of((i % blocks) * LN_ROWS, LN_ROWS)
            x = xbuf[t, pl.ds(start, LN_ROWS), :].astype(F32)
            y = norm_rows(x, vit_gain[...].reshape(1, DV))
            for j in range(F):
                normed[t, j, pl.ds(start, LN_ROWS), :] = y[:, j * C:(j + 1) * C].astype(BF16)
            return carry
        lax.fori_loop(lo_block, hi_block, body, 0)

    cuts = (3 * T * blocks // 8, 5 * T * blocks // 8)
    for c in ld_x:
        c.wait()
    norm_blocks(0, cuts[0])

    ld_wq.wait()
    arrive(0, r1)
    xq = jnp.concatenate([r1[j][0:T] for j in range(F)], axis=0)
    s2[...] = stack_halves(dot(xq.astype(BF16), wq[...])).astype(BF16)
    spread(2, s2, r2)
    arrive(1, rm)
    sm2[...] = total(rm, F)
    spread_z(0, sm2, rm2)
    norm_blocks(*cuts)
    head = lax.broadcasted_iota(jnp.int32, (R, HP, VW), 1)
    column = lax.broadcasted_iota(jnp.int32, (R, HP, VW), 2)
    own_head = (column >= head * VHD) & (column < (head + 1) * VHD)
    ld_wk.wait()
    arrive(2, r2)
    query = join_halves(total(r2, F).astype(BF16).astype(F32))

    spread_query = jnp.where(own_head, query[:, None, :], 0.0).reshape(R * HP, VW)
    folded = dot_t(spread_query.astype(BF16), wk[...]).astype(BF16)
    s3[...] = folded.reshape(F, T * HP, C)
    scatter(3, s3, r3)
    norm_blocks(cuts[1], T * blocks)
    arrive(3, r3)

    for t in range(T):
        by_token = dot_t(normed[t, 0], r3[0])
        for j in range(1, F):
            by_token = by_token + dot_t(normed[t, j], r3[j])
        scores = jnp.transpose(by_token)[t * HP:(t + 1) * HP]
        lifted = jnp.exp(scores / math.sqrt(VHD))
        probs = (lifted / jnp.sum(lifted, axis=-1, keepdims=True)).astype(BF16)
        for j in range(F):
            s4[j, pl.ds(t * HP, HP), :] = dot(probs, normed[t, j]).astype(BF16)
    scatter(4, s4, r4)
    ld_wv.wait()
    ld_wo.wait()
    arrive(4, r4)

    summed = dot(r4[...].reshape(R * HP, C), wv[...]).reshape(R, HP, VW)
    pooled_part = jnp.sum(jnp.where(own_head, summed, 0.0), axis=1)
    for j in range(F):
        s5[j, :, 0:PC] = pooled_part[:, j * PC:(j + 1) * PC]
    scatter(5, s5, r5)
    heads_dev = HC // (D // HEADS)
    hw = D // HEADS
    hr = (heads_dev, R, N)
    m_head = lax.broadcasted_iota(jnp.int32, hr, 0) + f * heads_dev
    m_row = lax.broadcasted_iota(jnp.int32, hr, 1) + z * R
    m_key = lax.broadcasted_iota(jnp.int32, hr, 2)
    segment = N // 4
    in_local = m_row // segment == m_key // segment
    in_dilated = (m_row % DILATION_STEP == m_head % DILATION_STEP) & (
        m_key % DILATION_STEP == m_head % DILATION_STEP)
    sets = jnp.where(in_local, 1.0, 0.0) + jnp.where(in_dilated, 1.0, 0.0)
    a_head = lax.broadcasted_iota(jnp.int32, (heads_dev, R, HC), 0)
    a_col = lax.broadcasted_iota(jnp.int32, (heads_dev, R, HC), 2)
    mine = (a_col >= a_head * hw) & (a_col < (a_head + 1) * hw)
    arrive(5, r5)
    pooled = total(r5, F)[:, :PC].astype(BF16)
    row_part = dot(pooled, wo[...])
    for j in range(F):
        s6[j] = row_part[:, j * C:(j + 1) * C]
    scatter(6, s6, r6)
    class_raw = jnp.concatenate([r1[j][T:2 * T] for j in range(F)], axis=0)
    ld_wp.wait()
    arrive(6, r6)
    class_row = (class_raw + total(r6, F)).astype(BF16)
    s7[...] = stack_halves(dot(class_row, wp[...])).astype(BF16)
    spread(7, s7, r7)

    arrive_z(0, rm2)
    all_meta = total(rm2, S)
    all_order = all_meta[0:1, 0:N]
    all_present = all_meta[1:2, 0:N].astype(F32)
    position = lax.broadcasted_iota(jnp.int32, (N, N), 0) + 1
    picker = jnp.where(position == all_order, 1.0, 0.0)
    place = lax.broadcasted_iota(jnp.int32, (N, 2 * N), 0) + 1
    pick_left = jnp.where(place == all_meta[2:3, 0:2 * N], 1.0, 0.0).astype(BF16)
    pick_right = jnp.where(place == all_meta[3:4, 0:2 * N], 1.0, 0.0).astype(BF16)
    key_present = dot_t(jnp.broadcast_to(all_present, (8, N)).astype(BF16), picker.astype(BF16))[0:1]

    allowed = (key_present.reshape(1, 1, N) > 0.5) | (m_row == m_key)
    times = jnp.where(allowed, sets, 0.0).reshape(heads_dev * R, N)
    arrive(7, r7)
    s8[...] = total(r7, F).astype(BF16)
    spread_z(1, s8, r8)
    ld_lg.wait()
    ld_lq.wait()
    ld_lk.wait()
    ld_lv.wait()
    ld_lo.wait()
    arrive_z(1, r8)

    every = r8[...].reshape(2 * N, D // 2)
    sequence = jnp.concatenate([dot(pick_left, every), dot(pick_right, every)], axis=1)
    lnormed = norm_rows(sequence, long_gain[...].reshape(1, D)).astype(BF16)
    projected = dot_t(lnormed, lqkv[...].reshape(3 * HC, D))
    qbuf[...] = projected[:, :HC]
    keys = projected[:, HC:2 * HC].astype(BF16)
    values = projected[:, 2 * HC:].astype(BF16)
    queries = qbuf[pl.ds(pl.multiple_of(z * R, R), R), :].astype(BF16).astype(F32)
    per_head = jnp.where(mine, queries[None], 0.0).reshape(heads_dev * R, HC).astype(BF16)
    lifted = jnp.exp(dot_t(per_head, keys) / math.sqrt(hw))
    weights = lifted.astype(BF16).astype(F32) * times
    denominator = jnp.sum(lifted * times, axis=-1, keepdims=True)
    mixed = dot(weights.astype(BF16), values) / denominator
    attended = jnp.sum(
        jnp.where(mine, mixed.reshape(heads_dev, R, HC), 0.0), axis=0).astype(BF16)
    terms = dot(attended, lo[...])
    for j in range(F):
        s9[j, :, 0:OC] = terms[:, j * OC:(j + 1) * OC]
    scatter(8, s9, r9)
    for j in range(F):
        seqc[j] = sequence[:, j * OC:(j + 1) * OC]
    residual = seqc[f, pl.ds(pl.multiple_of(z * R, R), R), :]
    for c in sends[:1 - F]:
        c.wait_send()
    arrive(8, r9)
    out[...] = (residual + total(r9, F)[:, :OC]).astype(BF16)
    for c in sends[1 - F:]:
        c.wait_send()


def local(
    tile_patches, vit_gain, w_query, w_key, w_value, w_out, w_proj,
    long_gain, long_query, long_key, long_value, long_out, seq_order, counts,
):
    long_query, long_key, long_value = long_query.T, long_key.T, long_value.T
    S = lax.axis_size("seq")
    F = lax.axis_size("fsdp")
    T, PATCH, DV = tile_patches.shape
    VW = w_key.shape[1]
    D = w_proj.shape[1]
    R, C, HC, OC, PC = T * F, DV // F, long_query.shape[0], D // F, VW // F
    HP = up(VW // VHD, 16)
    N = R * S
    L = up(2 * N, 128)
    V = pltpu.VMEM
    any_, vmem = pl.BlockSpec(memory_space=pl.ANY), pl.BlockSpec(memory_space=pltpu.VMEM)
    like = lambda a: V(a.shape, a.dtype)
    pair = lambda shape, dtype: [V((F,) + shape, dtype), V((F,) + shape, dtype)]
    fan = lambda n, shape, dtype: [V(shape, dtype), V((n,) + shape, dtype)]
    flops = 2 * (3 * R * HP * C * VW + 2 * T * HP * PATCH * DV + 3 * N * D * HC)
    return pl.pallas_call(
        functools.partial(kernel, F, S),
        out_shape=pltpu.VMEM((R, OC), BF16),
        in_specs=[any_, any_, any_, any_, any_, any_, any_, any_,
                  any_, any_, any_, any_, any_, pl.BlockSpec(memory_space=pltpu.SMEM)],
        out_specs=vmem,
        scratch_shapes=[
            pltpu.SMEM(seq_order.shape, jnp.int32), like(vit_gain), like(long_gain),
            V((T, 16, DV), BF16), like(tile_patches), V((T, F, PATCH, C), BF16),
            like(w_query), like(w_key), like(w_value), like(w_out), like(w_proj),
            V((3,) + long_query.shape, BF16), like(long_out),
            *pair((up(2 * T, 8), C), F32),
            *fan(F, (8, L), jnp.int32),
            *fan(S, (8, L), jnp.int32),
            *fan(F, (2 * R, VW // 2), BF16),
            *pair((T * HP, C), BF16),
            *pair((T * HP, C), BF16),
            *pair((R, up(PC, 128)), F32),
            *pair((R, C), F32),
            *fan(F, (2 * R, D // 2), BF16),
            *fan(S, (2 * R, D // 2), BF16),
            *pair((R, up(OC, 128)), F32),
            V((N, HC), F32), V((F, N, OC), F32),
            pltpu.SemaphoreType.DMA((13 + T,)),
            pltpu.SemaphoreType.DMA((9, F)), pltpu.SemaphoreType.DMA((9, F)),
            pltpu.SemaphoreType.DMA((2, S)), pltpu.SemaphoreType.DMA((2, S)),
        ],
        compiler_params=pltpu.CompilerParams(
            collective_id=0, has_side_effects=True, vmem_limit_bytes=60 * 2**20),
        cost_estimate=pl.CostEstimate(
            flops=flops, bytes_accessed=8 * 2**20, transcendentals=T * HP * PATCH),
    )(
        tile_patches, vit_gain, w_query, w_key, w_value, w_out, w_proj,
        long_gain, long_query, long_key, long_value, long_out,
        seq_order, counts,
    )


def solution(mesh):
    return jax.shard_map(
        local,
        mesh=mesh,
        in_specs=(
            P(("group", "seq", "fsdp"), None, None),
            P(),
            P("fsdp", None),
            P("fsdp", None),
            P("fsdp", None),
            P("fsdp", None),
            P("fsdp", None),
            P(),
            P(None, "fsdp"),
            P(None, "fsdp"),
            P(None, "fsdp"),
            P("fsdp", None),
            P(("group", "seq", "fsdp")),
            P(("group", "seq", "fsdp")),
        ),
        out_specs=P(("group", "seq"), "fsdp"),
        check_vma=False,
    )
```

```python
import functools
import math

import jax
import jax.numpy as jnp
from jax import lax
from jax.experimental import pallas as pl
from jax.experimental.pallas import tpu as pltpu
from jax.sharding import PartitionSpec as P

VHD = 64
HEADS = 16
DILATION_STEP = 4
EPSILON = 1e-06
LN_ROWS = 128
LN_PART = 16

F32 = jnp.float32
BF16 = jnp.bfloat16


def stack_halves(x):
    half = x.shape[1] // 2
    return jnp.concatenate([x[:, :half], x[:, half:]], axis=0)


def join_halves(x):
    half = x.shape[0] // 2
    return jnp.concatenate([x[:half], x[half:]], axis=1)


def up(n, m):
    return (n + m - 1) // m * m


def partners(me, n):
    if n % 2:
        return [lax.rem(me + k, n) for k in range(1, n)]
    pair, side = me // 2, me % 2
    found = []
    for k in range(1, n // 2):
        other = lax.rem(pair + k, n // 2) * 2
        found += [other + side, other + 1 - side]
    return found + [pair * 2 + 1 - side]


def norm_rows(x, gain):
    mean = jnp.mean(x, axis=-1, keepdims=True)
    centred = x - mean
    variance = jnp.mean(centred * centred, axis=-1, keepdims=True)
    return centred * lax.rsqrt(variance + EPSILON) * gain


def dot(a, b):
    return jnp.dot(a, b, preferred_element_type=F32)


def dot_t(a, b):
    return lax.dot_general(a, b, (((1,), (1,)), ((), ())), preferred_element_type=F32)


def kernel(
    F, S,
    patches, vit_gain_hbm, w_query, w_key, w_value, w_out, w_proj,
    long_gain_hbm, long_query, long_key, long_value, long_out, order_hbm, counts,
    out, order, vit_gain, long_gain,
    cls, xbuf, normed, wq, wk, wv, wo, wp, lqkv, lo,
    s1, r1, sm, rm, sm2, rm2, s2, r2, s3, r3, s4, r4, s5, r5, s6, r6, s7, r7,
    s8, r8, s9, r9, qbuf, seqc, sumbuf,
    lsem, fsend, frecv, zsend, zrecv,
):
    T, PATCH, DV = patches.shape
    VW = w_key.shape[1]
    D = w_proj.shape[1]
    R = T * F
    N = R * S
    C = DV // F
    HC = long_query.shape[0]
    OC = D // F
    PC = VW // F
    HP = up(VW // VHD, 16)
    f = lax.axis_index("fsdp")
    z = lax.axis_index("seq")

    loads = []

    def load(src, dst):
        c = pltpu.make_async_copy(src, dst, lsem.at[len(loads)])
        c.start()
        loads.append(c)
        return c

    ld_cls = load(patches.at[:, pl.ds(0, 16), :], cls)
    ld_vg = load(vit_gain_hbm, vit_gain)
    barrier = pltpu.get_barrier_semaphore()
    for k in range(1, F):
        pl.semaphore_signal(
            barrier, inc=1, device_id={"fsdp": lax.rem(f + k, F)},
            device_id_type=pl.DeviceIdType.MESH)
    for k in range(1, S):
        pl.semaphore_signal(
            barrier, inc=1, device_id={"seq": lax.rem(z + k, S)},
            device_id_type=pl.DeviceIdType.MESH)
    ld_order = load(order_hbm, order)
    ld_wq = load(w_query, wq)
    ld_x = [load(patches.at[t], xbuf.at[t]) for t in range(T)]
    ld_wk = load(w_key, wk)
    ld_wv = load(w_value, wv)
    ld_wo = load(w_out, wo)
    ld_wp = load(w_proj, wp)
    ld_lg = load(long_gain_hbm, long_gain)
    ld_lq = load(long_query, lqkv.at[0])
    ld_lk = load(long_key, lqkv.at[1])
    ld_lv = load(long_value, lqkv.at[2])
    ld_lo = load(long_out, lo)

    sends = []

    def push(hop, axis, me, n, src, dst, send_sems, recv_sems):
        for k, peer in enumerate(partners(me, n)):
            c = pltpu.make_async_remote_copy(
                src_ref=src(peer), dst_ref=dst.at[me],
                send_sem=send_sems.at[hop, k], recv_sem=recv_sems.at[hop, me],
                device_id={axis: peer}, device_id_type=pl.DeviceIdType.MESH)
            c.start()
            sends.append(c)

    def collect(hop, axis, me, n, dst, send_sems, recv_sems):
        for k, peer in enumerate(reversed(partners(me, n))):
            pltpu.make_async_remote_copy(
                src_ref=dst.at[me], dst_ref=dst.at[peer],
                send_sem=send_sems.at[hop, k], recv_sem=recv_sems.at[hop, peer],
                device_id={axis: peer}, device_id_type=pl.DeviceIdType.MESH,
            ).wait_recv()

    def scatter(hop, src, dst):
        push(hop, "fsdp", f, F, lambda peer: src.at[peer], dst, fsend, frecv)
        dst[f] = src[f]

    def spread(hop, src, dst):
        push(hop, "fsdp", f, F, lambda peer: src, dst, fsend, frecv)
        dst[f] = src[...]

    def spread_z(hop, src, dst):
        push(hop, "seq", z, S, lambda peer: src, dst, zsend, zrecv)
        dst[z] = src[...]

    def arrive(hop, dst):
        collect(hop, "fsdp", f, F, dst, fsend, frecv)

    def arrive_z(hop, dst):
        collect(hop, "seq", z, S, dst, zsend, zrecv)

    def total(ref, n):
        part = lambda j: ref[j].astype(F32) if ref.dtype == BF16 else ref[j]
        acc = part(0)
        for j in range(1, n):
            acc = acc + part(j)
        return acc

    ld_cls.wait()
    ld_vg.wait()
    raw = jnp.concatenate([cls[t, 0:8, :].astype(F32)[0:1] for t in range(T)], axis=0)
    class_normed = norm_rows(raw, vit_gain[...].reshape(1, DV)).astype(BF16).astype(F32)
    filler = s1.shape[1] - 2 * T
    packed = jnp.concatenate(
        [class_normed, raw, jnp.zeros((filler, DV), F32)], axis=0)
    for j in range(F):
        s1[j] = packed[:, j * C:(j + 1) * C]
    pl.semaphore_wait(barrier, F - 1 + S - 1)
    scatter(0, s1, r1)
    ld_order.wait()
    L = sm.shape[1]
    lane = lax.broadcasted_iota(jnp.int32, sm.shape, 1)
    row = lax.broadcasted_iota(jnp.int32, sm.shape, 0)
    meta = jnp.zeros(sm.shape, jnp.int32)
    first = z * R + f * T
    for t in range(T):
        here = jnp.where(t < counts[0], 1, 0)
        value = jnp.where(row == 0, order[t] + 1, jnp.where(row == 1, here, 0))
        meta = jnp.where(lane == first + t, value, meta)
        split = 2 * z * R + f * T + t + jnp.where(row == 3, R, 0)
        meta = jnp.where(
            (row >= 2) & (row < 4) & (lane == split), jnp.where(t < counts[0], order[t] + 1, 0), meta)
    sm[...] = meta
    spread(1, sm, rm)

    s5[...] = jnp.zeros(s5.shape, F32)
    s9[...] = jnp.zeros(s9.shape, F32)
    blocks = PATCH // LN_ROWS

    ones = jnp.full((DV, 128), 1.0, BF16)
    gain_row = vit_gain[...].reshape(1, DV)

    def norm_blocks(lo_block, hi_block):
        def body(i, carry):
            t = i // blocks
            base = pl.multiple_of((i % blocks) * LN_ROWS, LN_ROWS)
            sums = dot(xbuf[t, pl.ds(base, LN_ROWS), :], ones)
            for part in range(LN_ROWS // LN_PART):
                start = pl.multiple_of(base + part * LN_PART, LN_PART)
                x = xbuf[t, pl.ds(start, LN_PART), :].astype(F32)
                mean = sums[part * LN_PART:(part + 1) * LN_PART] / DV
                centred = x - jnp.concatenate([mean] * (DV // 128), axis=1)
                variance = jnp.mean(centred * centred, axis=-1, keepdims=True)
                y = centred * lax.rsqrt(variance + EPSILON) * gain_row
                for j in range(F):
                    normed[t, j, pl.ds(start, LN_PART), :] = y[:, j * C:(j + 1) * C].astype(BF16)
            return carry
        lax.fori_loop(lo_block, hi_block, body, 0)

    cuts = (T * blocks // 4, T * blocks // 2)
    for c in ld_x:
        c.wait()
    norm_blocks(0, cuts[0])

    ld_wq.wait()
    arrive(0, r1)
    xq = jnp.concatenate([r1[j][0:T] for j in range(F)], axis=0)
    s2[...] = stack_halves(dot(xq.astype(BF16), wq[...])).astype(BF16)
    spread(2, s2, r2)
    arrive(1, rm)
    sm2[...] = total(rm, F)
    spread_z(0, sm2, rm2)
    norm_blocks(*cuts)
    head = lax.broadcasted_iota(jnp.int32, (R, HP, VW), 1)
    column = lax.broadcasted_iota(jnp.int32, (R, HP, VW), 2)
    own_head = (column >= head * VHD) & (column < (head + 1) * VHD)
    ld_wk.wait()
    arrive(2, r2)
    query = join_halves(total(r2, F).astype(BF16).astype(F32))

    spread_query = jnp.where(own_head, query[:, None, :], 0.0).reshape(R * HP, VW)
    folded = dot_t(spread_query.astype(BF16), wk[...]).astype(BF16)
    s3[...] = folded.reshape(F, T * HP, C)
    scatter(3, s3, r3)
    norm_blocks(cuts[1], T * blocks)
    arrive(3, r3)

    for t in range(T):
        by_token = dot_t(normed[t, 0], r3[0])
        for j in range(1, F):
            by_token = by_token + dot_t(normed[t, j], r3[j])
        scores = jnp.transpose(by_token)[t * HP:(t + 1) * HP]
        lifted = jnp.exp(scores / math.sqrt(VHD))
        probs = (lifted / jnp.sum(lifted, axis=-1, keepdims=True)).astype(BF16)
        for j in range(F):
            s4[j, pl.ds(t * HP, HP), :] = dot(probs, normed[t, j]).astype(BF16)
    scatter(4, s4, r4)
    ld_wv.wait()
    ld_wo.wait()
    arrive(4, r4)

    summed = dot(r4[...].reshape(R * HP, C), wv[...])
    side = lax.broadcasted_iota(jnp.int32, (R, 2 * VHD), 1) < VHD
    pieces = []
    for c in range(VW // (2 * VHD)):
        sumbuf[c] = summed[:, c * 2 * VHD:(c + 1) * 2 * VHD]
        pieces.append(jnp.where(
            side,
            sumbuf[c, pl.ds(2 * c, R, stride=HP), :],
            sumbuf[c, pl.ds(2 * c + 1, R, stride=HP), :]))
    pooled_part = jnp.concatenate(pieces, axis=1)
    for j in range(F):
        s5[j, :, 0:PC] = pooled_part[:, j * PC:(j + 1) * PC]
    scatter(5, s5, r5)
    heads_dev = HC // (D // HEADS)
    hw = D // HEADS
    hr = (heads_dev, R, N)
    m_head = lax.broadcasted_iota(jnp.int32, hr, 0) + f * heads_dev
    m_row = lax.broadcasted_iota(jnp.int32, hr, 1) + z * R
    m_key = lax.broadcasted_iota(jnp.int32, hr, 2)
    segment = N // 4
    in_local = m_row // segment == m_key // segment
    in_dilated = (m_row % DILATION_STEP == m_head % DILATION_STEP) & (
        m_key % DILATION_STEP == m_head % DILATION_STEP)
    sets = jnp.where(in_local, 1.0, 0.0) + jnp.where(in_dilated, 1.0, 0.0)
    a_head = lax.broadcasted_iota(jnp.int32, (heads_dev, R, HC), 0)
    a_col = lax.broadcasted_iota(jnp.int32, (heads_dev, R, HC), 2)
    mine = (a_col >= a_head * hw) & (a_col < (a_head + 1) * hw)
    arrive(5, r5)
    pooled = total(r5, F)[:, :PC].astype(BF16)
    row_part = dot(pooled, wo[...])
    for j in range(F):
        s6[j] = row_part[:, j * C:(j + 1) * C]
    scatter(6, s6, r6)
    class_raw = jnp.concatenate([r1[j][T:2 * T] for j in range(F)], axis=0)
    ld_wp.wait()
    arrive(6, r6)
    class_row = (class_raw + total(r6, F)).astype(BF16)
    s7[...] = stack_halves(dot(class_row, wp[...])).astype(BF16)
    spread(7, s7, r7)

    arrive_z(0, rm2)
    all_meta = total(rm2, S)
    all_order = all_meta[0:1, 0:N]
    all_present = all_meta[1:2, 0:N].astype(F32)
    position = lax.broadcasted_iota(jnp.int32, (N, N), 0) + 1
    picker = jnp.where(position == all_order, 1.0, 0.0)
    place = lax.broadcasted_iota(jnp.int32, (N, 2 * N), 0) + 1
    pick_left = jnp.where(place == all_meta[2:3, 0:2 * N], 1.0, 0.0).astype(BF16)
    pick_right = jnp.where(place == all_meta[3:4, 0:2 * N], 1.0, 0.0).astype(BF16)
    key_present = dot_t(jnp.broadcast_to(all_present, (8, N)).astype(BF16), picker.astype(BF16))[0:1]

    allowed = (key_present.reshape(1, 1, N) > 0.5) | (m_row == m_key)
    times = jnp.where(allowed, sets, 0.0).reshape(heads_dev * R, N)
    arrive(7, r7)
    s8[...] = total(r7, F).astype(BF16)
    spread_z(1, s8, r8)
    ld_lg.wait()
    ld_lq.wait()
    ld_lk.wait()
    ld_lv.wait()
    ld_lo.wait()
    arrive_z(1, r8)

    every = r8[...].reshape(2 * N, D // 2)
    sequence = jnp.concatenate([dot(pick_left, every), dot(pick_right, every)], axis=1)
    lnormed = norm_rows(sequence, long_gain[...].reshape(1, D)).astype(BF16)
    projected = dot_t(lnormed, lqkv[...].reshape(3 * HC, D))
    qbuf[...] = projected[:, :HC]
    keys = projected[:, HC:2 * HC].astype(BF16)
    values = projected[:, 2 * HC:].astype(BF16)
    queries = qbuf[pl.ds(pl.multiple_of(z * R, R), R), :].astype(BF16).astype(F32)
    per_head = jnp.where(mine, queries[None], 0.0).reshape(heads_dev * R, HC).astype(BF16)
    lifted = jnp.exp(dot_t(per_head, keys) / math.sqrt(hw))
    weights = lifted.astype(BF16).astype(F32) * times
    denominator = jnp.sum(lifted * times, axis=-1, keepdims=True)
    mixed = dot(weights.astype(BF16), values) / denominator
    attended = jnp.sum(
        jnp.where(mine, mixed.reshape(heads_dev, R, HC), 0.0), axis=0).astype(BF16)
    terms = dot(attended, lo[...])
    for j in range(F):
        s9[j, :, 0:OC] = terms[:, j * OC:(j + 1) * OC]
    scatter(8, s9, r9)
    for j in range(F):
        seqc[j] = sequence[:, j * OC:(j + 1) * OC]
    residual = seqc[f, pl.ds(pl.multiple_of(z * R, R), R), :]
    for c in sends[:1 - F]:
        c.wait_send()
    arrive(8, r9)
    out[...] = (residual + total(r9, F)[:, :OC]).astype(BF16)
    for c in sends[1 - F:]:
        c.wait_send()


def local(
    tile_patches, vit_gain, w_query, w_key, w_value, w_out, w_proj,
    long_gain, long_query, long_key, long_value, long_out, seq_order, counts,
):
    long_query, long_key, long_value = long_query.T, long_key.T, long_value.T
    S = lax.axis_size("seq")
    F = lax.axis_size("fsdp")
    T, PATCH, DV = tile_patches.shape
    VW = w_key.shape[1]
    D = w_proj.shape[1]
    R, C, HC, OC, PC = T * F, DV // F, long_query.shape[0], D // F, VW // F
    HP = up(VW // VHD, 16)
    N = R * S
    L = up(2 * N, 128)
    V = pltpu.VMEM
    any_, vmem = pl.BlockSpec(memory_space=pl.ANY), pl.BlockSpec(memory_space=pltpu.VMEM)
    like = lambda a: V(a.shape, a.dtype)
    pair = lambda shape, dtype: [V((F,) + shape, dtype), V((F,) + shape, dtype)]
    fan = lambda n, shape, dtype: [V(shape, dtype), V((n,) + shape, dtype)]
    flops = 2 * (3 * R * HP * C * VW + 2 * T * HP * PATCH * DV + 3 * N * D * HC)
    return pl.pallas_call(
        functools.partial(kernel, F, S),
        out_shape=pltpu.VMEM((R, OC), BF16),
        in_specs=[any_, any_, any_, any_, any_, any_, any_, any_,
                  any_, any_, any_, any_, any_, pl.BlockSpec(memory_space=pltpu.SMEM)],
        out_specs=vmem,
        scratch_shapes=[
            pltpu.SMEM(seq_order.shape, jnp.int32), like(vit_gain), like(long_gain),
            V((T, 16, DV), BF16), like(tile_patches), V((T, F, PATCH, C), BF16),
            like(w_query), like(w_key), like(w_value), like(w_out), like(w_proj),
            V((3,) + long_query.shape, BF16), like(long_out),
            *pair((up(2 * T, 8), C), F32),
            *fan(F, (8, L), jnp.int32),
            *fan(S, (8, L), jnp.int32),
            *fan(F, (2 * R, VW // 2), BF16),
            *pair((T * HP, C), BF16),
            *pair((T * HP, C), BF16),
            *pair((R, up(PC, 128)), F32),
            *pair((R, C), F32),
            *fan(F, (2 * R, D // 2), BF16),
            *fan(S, (2 * R, D // 2), BF16),
            *pair((R, up(OC, 128)), F32),
            V((N, HC), F32), V((F, N, OC), F32), V((VW // (2 * VHD), R * HP, 2 * VHD), F32),
            pltpu.SemaphoreType.DMA((13 + T,)),
            pltpu.SemaphoreType.DMA((9, F)), pltpu.SemaphoreType.DMA((9, F)),
            pltpu.SemaphoreType.DMA((2, S)), pltpu.SemaphoreType.DMA((2, S)),
        ],
        compiler_params=pltpu.CompilerParams(
            collective_id=0, has_side_effects=True, vmem_limit_bytes=60 * 2**20),
        cost_estimate=pl.CostEstimate(
            flops=flops, bytes_accessed=8 * 2**20, transcendentals=T * HP * PATCH),
    )(
        tile_patches, vit_gain, w_query, w_key, w_value, w_out, w_proj,
        long_gain, long_query, long_key, long_value, long_out,
        seq_order, counts,
    )


def solution(mesh):
    return jax.shard_map(
        local,
        mesh=mesh,
        in_specs=(
            P(("group", "seq", "fsdp"), None, None),
            P(),
            P("fsdp", None),
            P("fsdp", None),
            P("fsdp", None),
            P("fsdp", None),
            P("fsdp", None),
            P(),
            P(None, "fsdp"),
            P(None, "fsdp"),
            P(None, "fsdp"),
            P("fsdp", None),
            P(("group", "seq", "fsdp")),
            P(("group", "seq", "fsdp")),
        ),
        out_specs=P(("group", "seq"), "fsdp"),
        check_vma=False,
    )
```

```python
import functools
import math

import jax
import jax.numpy as jnp
from jax import lax
from jax.experimental import pallas as pl
from jax.experimental.pallas import tpu as pltpu
from jax.sharding import PartitionSpec as P

VHD = 64
HEADS = 16
DILATION_STEP = 4
EPSILON = 1e-06
LN_ROWS = 128
LN_PART = 16

F32 = jnp.float32
BF16 = jnp.bfloat16


def stack_halves(x):
    half = x.shape[1] // 2
    return jnp.concatenate([x[:, :half], x[:, half:]], axis=0)


def join_halves(x):
    half = x.shape[0] // 2
    return jnp.concatenate([x[:half], x[half:]], axis=1)


def up(n, m):
    return (n + m - 1) // m * m


def partners(me, n):
    if n % 2:
        return [lax.rem(me + k, n) for k in range(1, n)]
    pair, side = me // 2, me % 2
    found = []
    for k in range(1, n // 2):
        other = lax.rem(pair + k, n // 2) * 2
        found += [other + side, other + 1 - side]
    return found + [pair * 2 + 1 - side]


def norm_rows(x, gain):
    mean = jnp.mean(x, axis=-1, keepdims=True)
    centred = x - mean
    variance = jnp.mean(centred * centred, axis=-1, keepdims=True)
    return centred * lax.rsqrt(variance + EPSILON) * gain


def dot(a, b):
    return jnp.dot(a, b, preferred_element_type=F32)


def dot_t(a, b):
    return lax.dot_general(a, b, (((1,), (1,)), ((), ())), preferred_element_type=F32)


def kernel(
    F, S,
    patches, vit_gain_hbm, w_query, w_key, w_value, w_out, w_proj,
    long_gain_hbm, long_query, long_key, long_value, long_out, order_hbm, counts,
    out, order, vit_gain, long_gain,
    cls, xbuf, normed, wq, wk, wv, wo, wp, lqkv, lo,
    s1, r1, sm, rm, sm2, rm2, s2, r2, s3, r3, s4, r4, s5, r5, s6, r6, s7, r7,
    s8, r8, s9, r9, qbuf, seqc, sumbuf,
    lsem, fsend, frecv, zsend, zrecv,
):
    T, PATCH, DV = patches.shape
    VW = w_key.shape[1]
    D = w_proj.shape[1]
    R = T * F
    N = R * S
    C = DV // F
    HC = long_query.shape[0]
    OC = D // F
    PC = VW // F
    HP = up(VW // VHD, 16)
    f = lax.axis_index("fsdp")
    z = lax.axis_index("seq")

    loads = []

    def load(src, dst):
        c = pltpu.make_async_copy(src, dst, lsem.at[len(loads)])
        c.start()
        loads.append(c)
        return c

    ld_cls = load(patches.at[:, pl.ds(0, 16), :], cls)
    ld_vg = load(vit_gain_hbm, vit_gain)
    barrier = pltpu.get_barrier_semaphore()
    for k in range(1, F):
        pl.semaphore_signal(
            barrier, inc=1, device_id={"fsdp": lax.rem(f + k, F)},
            device_id_type=pl.DeviceIdType.MESH)
    for k in range(1, S):
        pl.semaphore_signal(
            barrier, inc=1, device_id={"seq": lax.rem(z + k, S)},
            device_id_type=pl.DeviceIdType.MESH)
    ld_order = load(order_hbm, order)
    ld_wq = load(w_query, wq)
    ld_x = [load(patches.at[t], xbuf.at[t]) for t in range(T)]
    ld_wk = load(w_key, wk)
    ld_wv = load(w_value, wv)
    ld_wo = load(w_out, wo)
    ld_wp = load(w_proj, wp)
    ld_lg = load(long_gain_hbm, long_gain)
    ld_lq = load(long_query, lqkv.at[0])
    ld_lk = load(long_key, lqkv.at[1])
    ld_lv = load(long_value, lqkv.at[2])
    ld_lo = load(long_out, lo)

    sends = []

    def push(hop, axis, me, n, src, dst, send_sems, recv_sems):
        for k, peer in enumerate(partners(me, n)):
            c = pltpu.make_async_remote_copy(
                src_ref=src(peer), dst_ref=dst.at[me],
                send_sem=send_sems.at[hop, k], recv_sem=recv_sems.at[hop, me],
                device_id={axis: peer}, device_id_type=pl.DeviceIdType.MESH)
            c.start()
            sends.append(c)

    def collect(hop, axis, me, n, dst, send_sems, recv_sems):
        for k, peer in enumerate(reversed(partners(me, n))):
            pltpu.make_async_remote_copy(
                src_ref=dst.at[me], dst_ref=dst.at[peer],
                send_sem=send_sems.at[hop, k], recv_sem=recv_sems.at[hop, peer],
                device_id={axis: peer}, device_id_type=pl.DeviceIdType.MESH,
            ).wait_recv()

    def scatter(hop, src, dst):
        push(hop, "fsdp", f, F, lambda peer: src.at[peer], dst, fsend, frecv)
        dst[f] = src[f]

    def spread(hop, src, dst):
        push(hop, "fsdp", f, F, lambda peer: src, dst, fsend, frecv)
        dst[f] = src[...]

    def spread_z(hop, src, dst):
        push(hop, "seq", z, S, lambda peer: src, dst, zsend, zrecv)
        dst[z] = src[...]

    def arrive(hop, dst):
        collect(hop, "fsdp", f, F, dst, fsend, frecv)

    def arrive_z(hop, dst):
        collect(hop, "seq", z, S, dst, zsend, zrecv)

    def total(ref, n):
        part = lambda j: ref[j].astype(F32) if ref.dtype == BF16 else ref[j]
        acc = part(0)
        for j in range(1, n):
            acc = acc + part(j)
        return acc

    ld_cls.wait()
    ld_vg.wait()
    raw = jnp.concatenate([cls[t, 0:8, :].astype(F32)[0:1] for t in range(T)], axis=0)
    class_normed = norm_rows(raw, vit_gain[...].reshape(1, DV)).astype(BF16).astype(F32)
    filler = s1.shape[1] - 2 * T
    packed = jnp.concatenate(
        [class_normed, raw, jnp.zeros((filler, DV), F32)], axis=0)
    for j in range(F):
        s1[j] = packed[:, j * C:(j + 1) * C]
    pl.semaphore_wait(barrier, F - 1 + S - 1)
    scatter(0, s1, r1)
    ld_order.wait()
    L = sm.shape[1]
    lane = lax.broadcasted_iota(jnp.int32, sm.shape, 1)
    row = lax.broadcasted_iota(jnp.int32, sm.shape, 0)
    meta = jnp.zeros(sm.shape, jnp.int32)
    first = z * R + f * T
    for t in range(T):
        here = jnp.where(t < counts[0], 1, 0)
        value = jnp.where(row == 0, order[t] + 1, jnp.where(row == 1, here, 0))
        meta = jnp.where(lane == first + t, value, meta)
        split = 2 * z * R + f * T + t + jnp.where(row == 3, R, 0)
        meta = jnp.where(
            (row >= 2) & (row < 4) & (lane == split), jnp.where(t < counts[0], order[t] + 1, 0), meta)
    sm[...] = meta
    spread(1, sm, rm)

    s5[...] = jnp.zeros(s5.shape, F32)
    s9[...] = jnp.zeros(s9.shape, F32)
    blocks = PATCH // LN_ROWS

    ones = jnp.full((DV, 128), 1.0, BF16)
    gain_row = vit_gain[...].reshape(1, DV)

    def norm_blocks(lo_block, hi_block):
        def body(i, carry):
            t = i // blocks
            base = pl.multiple_of((i % blocks) * LN_ROWS, LN_ROWS)
            sums = dot(xbuf[t, pl.ds(base, LN_ROWS), :], ones)
            for part in range(LN_ROWS // LN_PART):
                start = pl.multiple_of(base + part * LN_PART, LN_PART)
                x = xbuf[t, pl.ds(start, LN_PART), :].astype(F32)
                mean = sums[part * LN_PART:(part + 1) * LN_PART] / DV
                centred = x - jnp.concatenate([mean] * (DV // 128), axis=1)
                variance = jnp.mean(centred * centred, axis=-1, keepdims=True)
                y = centred * lax.rsqrt(variance + EPSILON) * gain_row
                for j in range(F):
                    normed[t, j, pl.ds(start, LN_PART), :] = y[:, j * C:(j + 1) * C].astype(BF16)
            return carry
        lax.fori_loop(lo_block, hi_block, body, 0)

    cuts = (T * blocks // 4, T * blocks // 2)
    for c in ld_x:
        c.wait()
    norm_blocks(0, cuts[0])

    ld_wq.wait()
    arrive(0, r1)
    xq = jnp.concatenate([r1[j][0:T] for j in range(F)], axis=0)
    s2[...] = stack_halves(dot(xq.astype(BF16), wq[...])).astype(BF16)
    spread(2, s2, r2)
    arrive(1, rm)
    sm2[...] = total(rm, F)
    spread_z(0, sm2, rm2)
    norm_blocks(*cuts)
    head = lax.broadcasted_iota(jnp.int32, (R, HP, VW), 1)
    column = lax.broadcasted_iota(jnp.int32, (R, HP, VW), 2)
    own_head = (column >= head * VHD) & (column < (head + 1) * VHD)
    ld_wk.wait()
    arrive(2, r2)
    query = join_halves(total(r2, F).astype(BF16).astype(F32))

    spread_query = jnp.where(own_head, query[:, None, :], 0.0).reshape(R * HP, VW)
    folded = dot_t(spread_query.astype(BF16), wk[...]).astype(BF16)
    folded = folded.reshape(F, T, HP, C)
    for t in range(T):
        s3[t] = folded[:, t]
        scatter(9 + 2 * t, s3.at[t], r3.at[t])
    norm_blocks(cuts[1], T * blocks)
    for t in range(T):
        arrive(9 + 2 * t, r3.at[t])
        by_token = dot_t(normed[t, 0], r3[t, 0])
        for j in range(1, F):
            by_token = by_token + dot_t(normed[t, j], r3[t, j])
        scores = jnp.transpose(by_token)
        lifted = jnp.exp(scores / math.sqrt(VHD))
        probs = (lifted / jnp.sum(lifted, axis=-1, keepdims=True)).astype(BF16)
        for j in range(F):
            s4[t, j] = dot(probs, normed[t, j]).astype(BF16)
        scatter(10 + 2 * t, s4.at[t], r4.at[t])
    ld_wv.wait()
    ld_wo.wait()

    for t in range(T):
        arrive(10 + 2 * t, r4.at[t])
        summed = dot(r4[t].reshape(F * HP, C), wv[...])
        for c in range(VW // (2 * VHD)):
            for j in range(F):
                sumbuf[c, pl.ds((j * T + t) * HP, HP), :] = summed[
                    j * HP:(j + 1) * HP, c * 2 * VHD:(c + 1) * 2 * VHD]
    side = lax.broadcasted_iota(jnp.int32, (R, 2 * VHD), 1) < VHD
    pieces = []
    for c in range(VW // (2 * VHD)):
        pieces.append(jnp.where(
            side,
            sumbuf[c, pl.ds(2 * c, R, stride=HP), :],
            sumbuf[c, pl.ds(2 * c + 1, R, stride=HP), :]))
    pooled_part = jnp.concatenate(pieces, axis=1)
    for j in range(F):
        s5[j, :, 0:PC] = pooled_part[:, j * PC:(j + 1) * PC]
    scatter(5, s5, r5)
    heads_dev = HC // (D // HEADS)
    hw = D // HEADS
    hr = (heads_dev, R, N)
    m_head = lax.broadcasted_iota(jnp.int32, hr, 0) + f * heads_dev
    m_row = lax.broadcasted_iota(jnp.int32, hr, 1) + z * R
    m_key = lax.broadcasted_iota(jnp.int32, hr, 2)
    segment = N // 4
    in_local = m_row // segment == m_key // segment
    in_dilated = (m_row % DILATION_STEP == m_head % DILATION_STEP) & (
        m_key % DILATION_STEP == m_head % DILATION_STEP)
    sets = jnp.where(in_local, 1.0, 0.0) + jnp.where(in_dilated, 1.0, 0.0)
    a_head = lax.broadcasted_iota(jnp.int32, (heads_dev, R, HC), 0)
    a_col = lax.broadcasted_iota(jnp.int32, (heads_dev, R, HC), 2)
    mine = (a_col >= a_head * hw) & (a_col < (a_head + 1) * hw)
    arrive(5, r5)
    pooled = total(r5, F)[:, :PC].astype(BF16)
    row_part = dot(pooled, wo[...])
    for j in range(F):
        s6[j] = row_part[:, j * C:(j + 1) * C]
    scatter(6, s6, r6)
    class_raw = jnp.concatenate([r1[j][T:2 * T] for j in range(F)], axis=0)
    ld_wp.wait()
    arrive(6, r6)
    class_row = (class_raw + total(r6, F)).astype(BF16)
    s7[...] = stack_halves(dot(class_row, wp[...])).astype(BF16)
    spread(7, s7, r7)

    arrive_z(0, rm2)
    all_meta = total(rm2, S)
    all_order = all_meta[0:1, 0:N]
    all_present = all_meta[1:2, 0:N].astype(F32)
    position = lax.broadcasted_iota(jnp.int32, (N, N), 0) + 1
    picker = jnp.where(position == all_order, 1.0, 0.0)
    place = lax.broadcasted_iota(jnp.int32, (N, 2 * N), 0) + 1
    pick_left = jnp.where(place == all_meta[2:3, 0:2 * N], 1.0, 0.0).astype(BF16)
    pick_right = jnp.where(place == all_meta[3:4, 0:2 * N], 1.0, 0.0).astype(BF16)
    key_present = dot_t(jnp.broadcast_to(all_present, (8, N)).astype(BF16), picker.astype(BF16))[0:1]

    allowed = (key_present.reshape(1, 1, N) > 0.5) | (m_row == m_key)
    times = jnp.where(allowed, sets, 0.0).reshape(heads_dev * R, N)
    arrive(7, r7)
    s8[...] = total(r7, F).astype(BF16)
    spread_z(1, s8, r8)
    ld_lg.wait()
    ld_lq.wait()
    ld_lk.wait()
    ld_lv.wait()
    ld_lo.wait()
    arrive_z(1, r8)

    every = r8[...].reshape(2 * N, D // 2)
    sequence = jnp.concatenate([dot(pick_left, every), dot(pick_right, every)], axis=1)
    lnormed = norm_rows(sequence, long_gain[...].reshape(1, D)).astype(BF16)
    projected = dot_t(lnormed, lqkv[...].reshape(3 * HC, D))
    qbuf[...] = projected[:, :HC]
    keys = projected[:, HC:2 * HC].astype(BF16)
    values = projected[:, 2 * HC:].astype(BF16)
    queries = qbuf[pl.ds(pl.multiple_of(z * R, R), R), :].astype(BF16).astype(F32)
    per_head = jnp.where(mine, queries[None], 0.0).reshape(heads_dev * R, HC).astype(BF16)
    lifted = jnp.exp(dot_t(per_head, keys) / math.sqrt(hw))
    weights = lifted.astype(BF16).astype(F32) * times
    denominator = jnp.sum(lifted * times, axis=-1, keepdims=True)
    mixed = dot(weights.astype(BF16), values) / denominator
    attended = jnp.sum(
        jnp.where(mine, mixed.reshape(heads_dev, R, HC), 0.0), axis=0).astype(BF16)
    terms = dot(attended, lo[...])
    for j in range(F):
        s9[j, :, 0:OC] = terms[:, j * OC:(j + 1) * OC]
    scatter(8, s9, r9)
    for j in range(F):
        seqc[j] = sequence[:, j * OC:(j + 1) * OC]
    residual = seqc[f, pl.ds(pl.multiple_of(z * R, R), R), :]
    for c in sends[:1 - F]:
        c.wait_send()
    arrive(8, r9)
    out[...] = (residual + total(r9, F)[:, :OC]).astype(BF16)
    for c in sends[1 - F:]:
        c.wait_send()


def local(
    tile_patches, vit_gain, w_query, w_key, w_value, w_out, w_proj,
    long_gain, long_query, long_key, long_value, long_out, seq_order, counts,
):
    long_query, long_key, long_value = long_query.T, long_key.T, long_value.T
    S = lax.axis_size("seq")
    F = lax.axis_size("fsdp")
    T, PATCH, DV = tile_patches.shape
    VW = w_key.shape[1]
    D = w_proj.shape[1]
    R, C, HC, OC, PC = T * F, DV // F, long_query.shape[0], D // F, VW // F
    HP = up(VW // VHD, 16)
    N = R * S
    L = up(2 * N, 128)
    V = pltpu.VMEM
    any_, vmem = pl.BlockSpec(memory_space=pl.ANY), pl.BlockSpec(memory_space=pltpu.VMEM)
    like = lambda a: V(a.shape, a.dtype)
    pair = lambda shape, dtype: [V((F,) + shape, dtype), V((F,) + shape, dtype)]
    fan = lambda n, shape, dtype: [V(shape, dtype), V((n,) + shape, dtype)]
    flops = 2 * (3 * R * HP * C * VW + 2 * T * HP * PATCH * DV + 3 * N * D * HC)
    return pl.pallas_call(
        functools.partial(kernel, F, S),
        out_shape=pltpu.VMEM((R, OC), BF16),
        in_specs=[any_, any_, any_, any_, any_, any_, any_, any_,
                  any_, any_, any_, any_, any_, pl.BlockSpec(memory_space=pltpu.SMEM)],
        out_specs=vmem,
        scratch_shapes=[
            pltpu.SMEM(seq_order.shape, jnp.int32), like(vit_gain), like(long_gain),
            V((T, 16, DV), BF16), like(tile_patches), V((T, F, PATCH, C), BF16),
            like(w_query), like(w_key), like(w_value), like(w_out), like(w_proj),
            V((3,) + long_query.shape, BF16), like(long_out),
            *pair((up(2 * T, 8), C), F32),
            *fan(F, (8, L), jnp.int32),
            *fan(S, (8, L), jnp.int32),
            *fan(F, (2 * R, VW // 2), BF16),
            *[V((T, F, HP, C), BF16)] * 4,
            *pair((R, up(PC, 128)), F32),
            *pair((R, C), F32),
            *fan(F, (2 * R, D // 2), BF16),
            *fan(S, (2 * R, D // 2), BF16),
            *pair((R, up(OC, 128)), F32),
            V((N, HC), F32), V((F, N, OC), F32), V((VW // (2 * VHD), R * HP, 2 * VHD), F32),
            pltpu.SemaphoreType.DMA((13 + T,)),
            *[pltpu.SemaphoreType.DMA((9 + 2 * T, F))] * 2,
            pltpu.SemaphoreType.DMA((2, S)), pltpu.SemaphoreType.DMA((2, S)),
        ],
        compiler_params=pltpu.CompilerParams(
            collective_id=0, has_side_effects=True, vmem_limit_bytes=60 * 2**20),
        cost_estimate=pl.CostEstimate(
            flops=flops, bytes_accessed=8 * 2**20, transcendentals=T * HP * PATCH),
    )(
        tile_patches, vit_gain, w_query, w_key, w_value, w_out, w_proj,
        long_gain, long_query, long_key, long_value, long_out,
        seq_order, counts,
    )


def solution(mesh):
    return jax.shard_map(
        local,
        mesh=mesh,
        in_specs=(
            P(("group", "seq", "fsdp"), None, None),
            P(),
            P("fsdp", None),
            P("fsdp", None),
            P("fsdp", None),
            P("fsdp", None),
            P("fsdp", None),
            P(),
            P(None, "fsdp"),
            P(None, "fsdp"),
            P(None, "fsdp"),
            P("fsdp", None),
            P(("group", "seq", "fsdp")),
            P(("group", "seq", "fsdp")),
        ),
        out_specs=P(("group", "seq"), "fsdp"),
        check_vma=False,
    )
```
